32 devices in a mesh: space: 8 (over y, x, core), chan: 4 (over z).
Axes of the slice: x: 2, y: 2, z: 4, core: 2. Of those that a mesh axis runs over, the one named last changes fastest.
Arguments:
- activation: bfloat16 [8, 96, 16, 128], P('space', 'chan'), may hold values from -6 to 6
- weights: bfloat16 [3, 3, 3, 96, 96], replicated, may hold values from -0.125 to 0.125
- cotangent: bfloat16 [8, 96, 16, 128], P('space', 'chan'), may hold values from -6 to 6
Outputs:
- output: bfloat16 [8, 96, 16, 128], P('space', 'chan')
- input_grad: bfloat16 [8, 96, 16, 128], P('space', 'chan')
- weight_grad: float32 [3, 3, 3, 96, 96], P(None, None, None, None, 'chan')
The draws below stay inside these ranges and needn't reach their ends.
All inputs are finite; a program needn't handle non-finite values.
Results may differ from the reference program's by a relative error of at most 0.0095.
Values may be sent and summed in bfloat16 or wider, within the bound.
A program may use at most 64 MiB of HBM per device.

```python
import math
import jax
import jax.numpy as jnp
from jax import lax

C = 96
HEIGHT = 16
WIDTH = 128
DEPTH = 8


def level_of(stream_key, dims, cuts, least, largest):
    level, own = 1.0, jax.random.fold_in(stream_key, 6)
    for position, blocks in cuts:
        steps = jnp.exp(jax.random.uniform(jax.random.fold_in(own, position), (blocks,), jnp.float32, least / len(cuts), largest / len(cuts)))
        level = level * jnp.repeat(steps, dims[position] // blocks).reshape([-1 if axis == position else 1 for axis in range(len(dims))])
    return level


def normal_values(own_key, dims, spread, reach, pieces=(), kind=jnp.bfloat16):
    gain = level_of(own_key, dims, pieces, -0.22, 0.18) if pieces else 1.0
    values = jax.random.normal(own_key, dims, jnp.float32) * spread * gain
    return jnp.minimum(jnp.maximum(values, -reach), reach).astype(kind)


def setup_inputs(seed: int = 0) -> dict:
    seeds = jax.random.split(jax.random.key(seed), 4)
    activation = normal_values(seeds[0], (DEPTH, C, HEIGHT, WIDTH), 1.0, 6.0, ((0, 8), (1, 4)))
    weights = normal_values(seeds[1], (3, 3, 3, C, C), (27 * C) ** -0.5, 0.125)
    cotangent = normal_values(seeds[2], (DEPTH, C, HEIGHT, WIDTH), 1.0, 6.0, ((0, 8), (1, 4)))
    return dict(activation=activation, weights=weights, cotangent=cotangent)


def convolve(volume, kernel):
    return lax.conv_general_dilated(volume[None], kernel, (1, 1, 1), ((1, 1), (1, 1), (1, 1)), dimension_numbers=('NDCHW', 'DHWIO', 'NDCHW'), precision=lax.Precision.HIGHEST)[0]

def reference(activation, weights, cotangent):
    source = activation.astype(jnp.float32)
    kernel = weights.astype(jnp.float32)
    signal = cotangent.astype(jnp.float32)
    result, pullback = jax.vjp(convolve, source, kernel)
    source_grad, kernel_grad = pullback(signal)
    scaled = kernel_grad / math.sqrt(DEPTH * HEIGHT * WIDTH)
    return (result.astype(jnp.bfloat16), source_grad.astype(jnp.bfloat16), scaled)
```

```python
import functools
import math

import jax
import jax.numpy as jnp
from jax import lax
from jax.experimental import pallas as pl
from jax.experimental.pallas import tpu as pltpu
from jax.sharding import PartitionSpec as P

BF, F32 = jnp.bfloat16, jnp.float32
LANE = 128
ROWS_T = (((1,), (1,)), ((), ()))


def up_to(n, m):
    return -(-n // m) * m


def flip(i, m):
    out = i
    for b in range(m.bit_length()):
        if m >> b & 1:
            bit = lax.rem(lax.div(i, 1 << b), 2)
            out = out + (1 << b) * (1 - 2 * bit)
    return out


def kernel(space, chan, blk, pad, channels, height, groups, scale,
           a_hbm, g_hbm, w_hbm, out_ref, back_ref, wg_ref,
           ga, gv, w_ref, x3, xg, wt, wf, wb, z32, t32, r32, part,
           halo, psend, precv, wflat, csend, crecv, wall, acc, place_q,
           rsend, rrecv,
           l_s, g_s, g_r, h_s, h_r, p_s, p_r, c_s, c_r, w_s, w_r, r_s, r_r):
    e = lax.axis_index("space")
    z = lax.axis_index("chan")
    rows = blk * height
    span = height * LANE
    per = chan // groups
    half, gl = wall.shape[2], wall.shape[3]
    some = -(-blk // 8) * 8
    wide = acc.shape[1] // 3
    up, down = lax.rem(e + 1, space), lax.rem(e + space - 1, space)
    core = lax.rem(e, 2)

    barrier = pltpu.get_barrier_semaphore()
    others = [{"chan": flip(z, k)} for k in range(1, chan)]
    others += [{"space": flip(e, k)} for k in range(1, space)]
    for other in others:
        pl.semaphore_signal(barrier, inc=1, device_id=other)
    loads = [pltpu.make_async_copy(g_hbm, gv, l_s.at[0]),
             pltpu.make_async_copy(a_hbm, ga.at[0], l_s.at[1]),
             pltpu.make_async_copy(w_hbm, w_ref, l_s.at[2])]
    for c in loads:
        c.start()

    def send(src, dst, ssem, rsem, to):
        return pltpu.make_async_remote_copy(src, dst, ssem, rsem, device_id=to)

    gathers = [None] + [
        send(a_hbm, ga.at[k], g_s.at[k], g_r.at[k], {"chan": flip(z, k)})
        for k in range(1, chan)]
    halo_up = send(g_hbm, halo.at[0], h_s.at[0], h_r.at[0], {"space": up})
    halo_down = send(g_hbm, halo.at[1], h_s.at[1], h_r.at[1], {"space": down})
    has_up, has_down = e < space - 1, e > 0

    pl.semaphore_wait(barrier, len(others))
    for c in gathers[1:]:
        c.start()
    pl.when(has_up)(halo_up.start)
    pl.when(has_down)(halo_down.start)

    def no_lower():
        halo[0] = jnp.zeros((rows, LANE), BF)
        precv[0] = jnp.zeros((rows, LANE), BF)

    def no_upper():
        halo[1] = jnp.zeros((rows, LANE), BF)
        precv[1] = jnp.zeros((rows, LANE), BF)

    pl.when(e == 0)(no_lower)
    pl.when(e == space - 1)(no_upper)

    z32[...] = jnp.zeros_like(z32)
    x3[:, 0:LANE] = jnp.zeros((x3.shape[0], LANE), BF)
    x3[:, span + LANE:span + 2 * LANE] = jnp.zeros((x3.shape[0], LANE), BF)
    wflat[...] = jnp.zeros_like(wflat)
    few = lax.broadcasted_iota(jnp.int32, (rows, LANE), 1)

    def fill(dst, row_of, first, src):
        v = src.astype(F32)
        z32[0, 0:rows, :] = jnp.where(few == 0, 0.0, pltpu.roll(v, 1, 1))
        z32[1, 0:rows, :] = v
        z32[2, 0:rows, :] = jnp.where(few == LANE - 1, 0.0, pltpu.roll(v, LANE - 1, 1))
        for c in range(3):
            at = row_of(c)
            for h in range(height):
                dst[at:at + pad, (h + first) * LANE:(h + first + 1) * LANE] = (
                    z32[c, pl.ds(h, pad, stride=height), :].astype(BF))

    def fill_signal(a, src):
        fill(xg, lambda c: (c * 3 + a) * pad, 0, src)

    def fill_source(k):
        fill(x3, lambda c: (k * 3 + c) * pad, 1, ga[k])

    loads[0].wait()
    fill_signal(1, gv[...])
    loads[1].wait()
    fill_source(0)

    loads[2].wait()
    thick = 9 * pad
    first = lax.broadcasted_iota(jnp.int32, (channels, thick), 0) - z * blk
    place = lax.broadcasted_iota(jnp.int32, (channels, thick), 1)
    inside = (first >= 0) & (first < blk)
    for b in range(3):
        total = jnp.zeros((channels, thick), F32)
        for c in range(3):
            for a in range(3):
                spot = inside & (place == first + (c * 3 + a) * pad)
                tap = w_ref[(a * 3 + 2 - b) * 3 + 2 - c]
                total = total + jnp.dot(
                    tap, jnp.where(spot, 1.0, 0.0).astype(BF), preferred_element_type=F32)
        wb[b * channels:(b + 1) * channels, :] = total.astype(BF)

    row = lax.broadcasted_iota(jnp.int32, (pad, channels), 0)
    col = lax.broadcasted_iota(jnp.int32, (pad, channels), 1)
    pick = jnp.where((col == row + z * blk) & (row < blk), 1.0, 0.0).astype(BF)
    for a in range(3):
        for b in range(3):
            for c in range(3):
                at = (b * 3 + a) * pad
                wt[c, at:at + pad, :] = lax.dot_general(
                    pick, w_ref[(a * 3 + b) * 3 + c], ROWS_T,
                    preferred_element_type=F32).astype(BF)
    deep = 3 * pad * chan
    channel = lax.broadcasted_iota(jnp.int32, (channels, deep), 0)
    spot = lax.broadcasted_iota(jnp.int32, (channels, deep), 1)
    goes = jnp.zeros((channels, deep), jnp.int32)
    for k in range(chan):
        local = channel - flip(z, k) * blk
        goes = jnp.where((local >= 0) & (local < blk), local + k * 3 * pad, goes)
    total = jnp.zeros((9 * pad, deep), F32)
    for c in range(3):
        total = total + jnp.dot(
            wt[c], jnp.where(spot == goes + c * pad, 1.0, 0.0).astype(BF),
            preferred_element_type=F32)
    wf[...] = total.astype(BF)

    place_q[...] = jnp.zeros_like(place_q)
    row = lax.broadcasted_iota(jnp.int32, (pad, wide), 0)
    col = lax.broadcasted_iota(jnp.int32, (pad, wide), 1)
    for k in range(chan):
        hit = (row < blk) & (col == row + flip(z, k) * blk)
        block = jnp.where(hit, 1.0, 0.0).astype(BF)
        for c in range(3):
            at = ((k % per) * 3 + c) * pad
            place_q[k // per, at:at + pad, c * wide:(c + 1) * wide] = block

    pairs = [send(csend.at[k], crecv.at[k], c_s.at[k], c_r.at[k], {"space": flip(e, 1)})
             for k in range(groups)]
    shares = [[send(wall.at[k, e], wall.at[k, e], w_s.at[k, m], w_r.at[k, m],
                    {"space": flip(e, m)}) for m in range(1, space)]
              for k in range(groups)]

    def my_half(k, which):
        return wflat[k, pl.ds(pl.multiple_of(which * half, 16), half), :]

    def share(k):
        many = per * 3 * pad
        for b in range(3):
            one = lax.dot_general(
                xg[3 * pad:6 * pad, :],
                x3[k * many:(k + 1) * many, b * LANE:b * LANE + span],
                ROWS_T, preferred_element_type=F32)
            for a in range(3):
                at = (b * 3 + a) * some
                wflat[k, at:at + some, 0:many] = one[a * pad:a * pad + some, :]
        csend[k] = my_half(k, 1 - core).astype(BF)
        pairs[k].start()

    def spread(k):
        pairs[k].wait_recv()
        wall[k, e] = (my_half(k, core) + crecv[k].astype(F32)).astype(BF)
        for c in shares[k]:
            c.start()

    def collect(k):
        for c in shares[k]:
            c.wait_recv()
        for side in range(2):
            total = wall[k, side].astype(F32)
            for chip in range(1, space // 2):
                total = total + wall[k, 2 * chip + side].astype(F32)
            moved = jnp.dot(total.astype(BF), place_q[k], preferred_element_type=F32)
            at = side * half
            acc[at:at + half, :] = moved if k == 0 else acc[at:at + half, :] + moved

    pl.when(has_down)(halo_up.wait_recv)
    fill_signal(2, halo[0])
    pl.when(has_up)(halo_down.wait_recv)
    fill_signal(0, halo[1])
    for k in range(1, per):
        gathers[k].wait_recv()
        fill_source(k)
    share(0)

    def shifted(count, first_row, group, h):
        def piece(b, hh):
            at = first_row + b * group
            return r32[at:at + count, hh * LANE:(hh + 1) * LANE]
        v = piece(1, h)
        if h > 0:
            v = v + piece(0, h - 1)
        if h < height - 1:
            v = v + piece(2, h + 1)
        return v

    r32[0:3 * channels, :] = jnp.dot(wb[...], xg[...], preferred_element_type=F32)
    spread(0)
    for h in range(height):
        part[pl.ds(h, channels, stride=height), :] = shifted(channels, 0, channels, h)

    sums = [send(rsend.at[k], rrecv.at[k], r_s.at[k], r_r.at[k], {"chan": flip(z, k)})
            for k in range(1, chan)]

    def block_of(t):
        return part[pl.ds(pl.multiple_of(t * rows, 16), rows), :]

    for k in range(1, chan):
        rsend[k] = block_of(flip(z, k)).astype(BF)

    for group in range(1, groups):
        for k in range(group * per, (group + 1) * per):
            gathers[k].wait_recv()
            if k == chan - 1:
                for c in sums:
                    c.start()
            fill_source(k)
        share(group)
        if group < groups - 1:
            spread(group)

    r32[0:9 * pad, :] = jnp.dot(wf[...], x3[:, LANE:LANE + span], preferred_element_type=F32)
    if groups > 1:
        spread(groups - 1)

    def relay(a):
        for h in range(height):
            t32[a, pl.ds(h, pad, stride=height), :] = shifted(pad, a * pad, 3 * pad, h)

    relay(0)
    psend[0] = t32[0, 0:rows, :].astype(BF)
    pair = (send(psend.at[0], precv.at[0], p_s.at[0], p_r.at[0], {"space": up}),
            send(psend.at[1], precv.at[1], p_s.at[1], p_r.at[1], {"space": down}))
    pl.when(has_up)(pair[0].start)
    relay(2)
    psend[1] = t32[2, 0:rows, :].astype(BF)
    pl.when(has_down)(pair[1].start)
    relay(1)

    for k in range(groups):
        collect(k)
    for a in range(3):
        for b in range(3):
            for c in range(3):
                at = (b * 3 + a) * some
                wg_ref[(a * 3 + b) * 3 + c] = (
                    acc[at:at + blk, c * wide:c * wide + channels] * scale)

    pl.when(has_down)(pair[0].wait_recv)
    pl.when(has_up)(pair[1].wait_recv)
    out_ref[...] = (t32[1, 0:rows, :] + precv[0].astype(F32)
                    + precv[1].astype(F32)).astype(BF)

    for c in sums:
        c.wait_recv()
    total = block_of(z)
    for k in range(1, chan):
        total = total + rrecv[k].astype(F32)
    back_ref[...] = total.astype(BF)

    for c in gathers[1:] + sums + pairs:
        c.wait_send()
    for group in shares:
        for c in group:
            c.wait_send()
    for c in (halo_up, pair[0]):
        pl.when(has_up)(c.wait_send)
    for c in (halo_down, pair[1]):
        pl.when(has_down)(c.wait_send)


def write(*refs):
    n = len(refs) // 2
    copies = [pltpu.make_async_copy(refs[i], refs[n + i], refs[-1].at[i]) for i in range(n)]
    for c in copies:
        c.start()
    for c in copies:
        c.wait()


def body(space, chan, activation, weights, cotangent):
    planes, blk, height, width = activation.shape
    channels = weights.shape[3]
    assert planes == 1 and width == LANE
    pad = up_to(blk, 16)
    rows = blk * height
    groups = min(chan, 4)
    scale = 1.0 / math.sqrt(planes * space * height * width)
    dma = pltpu.SemaphoreType.DMA
    vm = pltpu.VMEM
    deep = 3 * pad * chan
    gl = up_to(deep // groups, LANE)
    some = up_to(blk, 8)
    half = up_to(9 * some, 32) // 2
    wide = up_to(channels, LANE)
    shapes = (
        jax.ShapeDtypeStruct((rows, LANE), BF),
        jax.ShapeDtypeStruct((rows, LANE), BF),
        jax.ShapeDtypeStruct((27, blk, channels), F32),
    )
    outs = pl.pallas_call(
        functools.partial(kernel, space, chan, blk, pad, channels, height, groups, scale),
        out_shape=shapes,
        in_specs=[pl.BlockSpec(memory_space=pltpu.HBM)] * 3,
        out_specs=[pl.BlockSpec(memory_space=vm)] * 3,
        scratch_shapes=[
            vm((chan, rows, LANE), BF),
            vm((rows, LANE), BF),
            vm((27, channels, channels), BF),
            vm((deep, (height + 2) * LANE), BF),
            vm((9 * pad, height * LANE), BF),
            vm((3, 9 * pad, channels), BF),
            vm((9 * pad, deep), BF),
            vm((3 * channels, 9 * pad), BF),
            vm((3, pad * height, LANE), F32),
            vm((3, pad * height, LANE), F32),
            vm((max(9 * pad, 3 * channels), height * LANE), F32),
            vm((channels * height, LANE), F32),
            vm((2, rows, LANE), BF),
            vm((2, rows, LANE), BF),
            vm((2, rows, LANE), BF),
            vm((groups, 2 * half, gl), F32),
            vm((groups, half, gl), BF),
            vm((groups, half, gl), BF),
            vm((groups, space, half, gl), BF),
            vm((2 * half, 3 * wide), F32),
            vm((groups, gl, 3 * wide), BF),
            vm((chan, rows, LANE), BF),
            vm((chan, rows, LANE), BF),
            dma((3,)), dma((chan,)), dma((chan,)), dma((2,)), dma((2,)), dma((2,)), dma((2,)),
            dma((groups,)), dma((groups,)), dma((groups, space)), dma((groups, space)),
            dma((chan,)), dma((chan,)),
        ],
        compiler_params=pltpu.CompilerParams(
            collective_id=0, has_side_effects=True, vmem_limit_bytes=40 * 2**20),
    )(*[pltpu.with_memory_space_constraint(x, pltpu.HBM) for x in (
        activation.reshape(rows, width), cotangent.reshape(rows, width),
        weights.reshape(27, channels, channels))])
    out, back, grads = pl.pallas_call(
        write,
        out_shape=shapes,
        in_specs=[pl.BlockSpec(memory_space=vm)] * 3,
        out_specs=[pl.BlockSpec(memory_space=pltpu.HBM)] * 3,
        scratch_shapes=[dma((3,))],
        compiler_params=pltpu.CompilerParams(vmem_limit_bytes=2**20),
    )(*outs)
    field = (1, blk, height, width)
    grads = jnp.swapaxes(grads.reshape(3, 3, 3, blk, channels), 3, 4)
    return out.reshape(field), back.reshape(field), grads


def solution(mesh):
    field = P("space", "chan", None, None)
    return jax.shard_map(
        functools.partial(body, mesh.shape["space"], mesh.shape["chan"]),
        mesh=mesh,
        in_specs=(field, P(), field),
        out_specs=(field, field, P(None, None, None, None, "chan")),
        check_vma=False,
    )
```

```python
import functools
import math

import jax
import jax.numpy as jnp
from jax import lax
from jax.experimental import pallas as pl
from jax.experimental.pallas import tpu as pltpu
from jax.sharding import PartitionSpec as P

BF, F32 = jnp.bfloat16, jnp.float32
LANE = 128
ROWS_T = (((1,), (1,)), ((), ()))


def up_to(n, m):
    return -(-n // m) * m


def flip(i, m):
    out = i
    for b in range(m.bit_length()):
        if m >> b & 1:
            bit = lax.rem(lax.div(i, 1 << b), 2)
            out = out + (1 << b) * (1 - 2 * bit)
    return out


def kernel(space, chan, blk, pad, channels, height, groups, scale,
           a_hbm, g_hbm, w_hbm, out_ref, back_ref, wg_ref,
           ga, gv, w_ref, x3, xg, wt, wf, wb, z32, t32, r32, part,
           halo, psend, precv, wflat, csend, crecv, wall, full, stack, acc, place_q,
           rsend, rrecv,
           l_s, g_s, g_r, h_s, h_r, p_s, p_r, c_s, c_r, w_s, w_r, f_s, f_r, r_s, r_r):
    e = lax.axis_index("space")
    z = lax.axis_index("chan")
    rows = blk * height
    span = height * LANE
    per = chan // groups
    tall, half = wall.shape[2], wall.shape[3]
    some = up_to(blk, 8)
    ring = up_to(3 * some, 16)
    each = 3 * some if per == 1 else per * ring
    wide = acc.shape[1] // 3
    up, down = lax.rem(e + 1, space), lax.rem(e + space - 1, space)
    core = lax.rem(e, 2)

    barrier = pltpu.get_barrier_semaphore()
    others = [{"chan": flip(z, k)} for k in range(1, chan)]
    others += [{"space": flip(e, k)} for k in range(1, space)]
    for other in others:
        pl.semaphore_signal(barrier, inc=1, device_id=other)
    loads = [pltpu.make_async_copy(g_hbm, gv, l_s.at[0]),
             pltpu.make_async_copy(a_hbm, ga.at[0], l_s.at[1]),
             pltpu.make_async_copy(w_hbm, w_ref, l_s.at[2])]
    for c in loads:
        c.start()

    def send(src, dst, ssem, rsem, to):
        return pltpu.make_async_remote_copy(src, dst, ssem, rsem, device_id=to)

    gathers = [None] + [
        send(a_hbm, ga.at[k], g_s.at[k], g_r.at[k], {"chan": flip(z, k)})
        for k in range(1, chan)]
    halo_up = send(g_hbm, halo.at[0], h_s.at[0], h_r.at[0], {"space": up})
    halo_down = send(g_hbm, halo.at[1], h_s.at[1], h_r.at[1], {"space": down})
    has_up, has_down = e < space - 1, e > 0

    pl.semaphore_wait(barrier, len(others))
    for c in gathers[1:]:
        c.start()
    pl.when(has_up)(halo_up.start)
    pl.when(has_down)(halo_down.start)

    def no_lower():
        halo[0] = jnp.zeros((rows, LANE), BF)
        precv[0] = jnp.zeros((rows, LANE), BF)

    def no_upper():
        halo[1] = jnp.zeros((rows, LANE), BF)
        precv[1] = jnp.zeros((rows, LANE), BF)

    pl.when(e == 0)(no_lower)
    pl.when(e == space - 1)(no_upper)

    z32[...] = jnp.zeros_like(z32)
    x3[:, 0:LANE] = jnp.zeros((x3.shape[0], LANE), BF)
    x3[:, span + LANE:span + 2 * LANE] = jnp.zeros((x3.shape[0], LANE), BF)
    wflat[...] = jnp.zeros_like(wflat)
    few = lax.broadcasted_iota(jnp.int32, (rows, LANE), 1)

    def shift(src):
        v = src.astype(F32)
        z32[0, 0:rows, :] = jnp.where(few == 0, 0.0, pltpu.roll(v, 1, 1))
        z32[1, 0:rows, :] = v
        z32[2, 0:rows, :] = jnp.where(few == LANE - 1, 0.0, pltpu.roll(v, LANE - 1, 1))

    def fill_signal(a, src):
        shift(src)
        for c in range(3):
            at = (c * 3 + a) * pad
            for h in range(height):
                xg[at:at + pad, h * LANE:(h + 1) * LANE] = (
                    z32[c, pl.ds(h, pad, stride=height), :].astype(BF))

    def fill_source(k):
        shift(ga[k])
        rest = [jnp.zeros((ring - 3 * some, LANE), F32)] if ring > 3 * some else []
        for h in range(height):
            taps = [z32[c, pl.ds(h, some, stride=height), :] for c in range(3)]
            x3[k * ring:(k + 1) * ring, (h + 1) * LANE:(h + 2) * LANE] = (
                jnp.concatenate(taps + rest, axis=0).astype(BF))

    loads[0].wait()
    fill_signal(1, gv[...])
    loads[1].wait()
    fill_source(0)

    loads[2].wait()
    thick = 9 * pad
    first = lax.broadcasted_iota(jnp.int32, (channels, thick), 0) - z * blk
    place = lax.broadcasted_iota(jnp.int32, (channels, thick), 1)
    inside = (first >= 0) & (first < blk)
    for b in range(3):
        total = jnp.zeros((channels, thick), F32)
        for c in range(3):
            for a in range(3):
                spot = inside & (place == first + (c * 3 + a) * pad)
                tap = w_ref[(a * 3 + 2 - b) * 3 + 2 - c]
                total = total + jnp.dot(
                    tap, jnp.where(spot, 1.0, 0.0).astype(BF), preferred_element_type=F32)
        wb[b * channels:(b + 1) * channels, :] = total.astype(BF)

    row = lax.broadcasted_iota(jnp.int32, (pad, channels), 0)
    col = lax.broadcasted_iota(jnp.int32, (pad, channels), 1)
    pick = jnp.where((col == row + z * blk) & (row < blk), 1.0, 0.0).astype(BF)
    for a in range(3):
        for b in range(3):
            for c in range(3):
                at = (b * 3 + a) * pad
                wt[c, at:at + pad, :] = lax.dot_general(
                    pick, w_ref[(a * 3 + b) * 3 + c], ROWS_T,
                    preferred_element_type=F32).astype(BF)
    deep = x3.shape[0]
    channel = lax.broadcasted_iota(jnp.int32, (channels, deep), 0)
    spot = lax.broadcasted_iota(jnp.int32, (channels, deep), 1)
    goes = jnp.zeros((channels, deep), jnp.int32)
    for k in range(chan):
        local = channel - flip(z, k) * blk
        goes = jnp.where((local >= 0) & (local < blk), local + k * ring, goes)
    total = jnp.zeros((9 * pad, deep), F32)
    for c in range(3):
        total = total + jnp.dot(
            wt[c], jnp.where(spot == goes + c * some, 1.0, 0.0).astype(BF),
            preferred_element_type=F32)
    wf[...] = total.astype(BF)

    place_q[...] = jnp.zeros_like(place_q)
    row = lax.broadcasted_iota(jnp.int32, (ring, wide), 0)
    col = lax.broadcasted_iota(jnp.int32, (ring, wide), 1)
    for k in range(chan):
        at = (k % per) * ring
        for c in range(3):
            own = row - c * some
            hit = (own >= 0) & (own < blk) & (col == own + flip(z, k) * blk)
            place_q[k // per, at:at + ring, c * wide:(c + 1) * wide] = (
                jnp.where(hit, 1.0, 0.0).astype(BF))

    pairs = [send(csend.at[k], crecv.at[k], c_s.at[k], c_r.at[k], {"space": flip(e, 1)})
             for k in range(groups)]
    shares = [[send(wall.at[k, e], wall.at[k, e], w_s.at[k, m], w_r.at[k, m],
                    {"space": flip(e, m)})
               for m in range(1 if k == groups - 1 else 2, space, 1 if k == groups - 1 else 2)]
              for k in range(groups)]
    passes = [send(full.at[k, core], full.at[k, core], f_s.at[k], f_r.at[k],
                   {"space": flip(e, 1)}) for k in range(groups - 1)]

    def my_half(k, which):
        return wflat[k, :, pl.ds(pl.multiple_of(which * half, LANE), half)]

    def share(k):
        many = per * ring
        for b in range(3):
            one = lax.dot_general(
                xg[3 * pad:6 * pad, :],
                x3[k * many:(k + 1) * many, b * LANE:b * LANE + span],
                ROWS_T, preferred_element_type=F32)
            for a in range(3):
                wflat[k, a * some:(a + 1) * some, b * each:(b + 1) * each] = (
                    one[a * pad:a * pad + some, 0:each])
        csend[k] = my_half(k, 1 - core).astype(BF)
        pairs[k].start()

    def spread(k):
        pairs[k].wait_recv()
        wall[k, e] = (my_half(k, core) + crecv[k].astype(F32)).astype(BF)
        for c in shares[k]:
            c.start()

    def summed(k, side):
        total = wall[k, side].astype(F32)
        for chip in range(1, space // 2):
            total = total + wall[k, 2 * chip + side].astype(F32)
        return total.astype(BF)

    def gather_up(k):
        for c in shares[k]:
            c.wait_recv()
        if k == groups - 1:
            for side in range(2):
                full[k, side] = summed(k, side)
        else:
            full[k, core] = summed(k, core)
            passes[k].start()

    def collect(k):
        if k < groups - 1:
            passes[k].wait_recv()
        both = jnp.concatenate([full[k, 0], full[k, 1]], axis=1)
        for b in range(3):
            stack[b * tall:(b + 1) * tall, 0:each] = both[:, b * each:(b + 1) * each]
        moved = jnp.dot(stack[...], place_q[k], preferred_element_type=F32)
        acc[...] = moved if k == 0 else acc[...] + moved

    pl.when(has_down)(halo_up.wait_recv)
    fill_signal(2, halo[0])
    pl.when(has_up)(halo_down.wait_recv)
    fill_signal(0, halo[1])
    for k in range(1, per):
        gathers[k].wait_recv()
        fill_source(k)
    share(0)

    def shifted(count, first_row, group, h):
        def piece(b, hh):
            at = first_row + b * group
            return r32[at:at + count, hh * LANE:(hh + 1) * LANE]
        v = piece(1, h)
        if h > 0:
            v = v + piece(0, h - 1)
        if h < height - 1:
            v = v + piece(2, h + 1)
        return v

    r32[0:3 * channels, :] = jnp.dot(wb[...], xg[...], preferred_element_type=F32)
    spread(0)
    for h in range(height):
        part[pl.ds(h, channels, stride=height), :] = shifted(channels, 0, channels, h)

    sums = [send(rsend.at[k], rrecv.at[k], r_s.at[k], r_r.at[k], {"chan": flip(z, k)})
            for k in range(1, chan)]

    def block_of(t):
        return part[pl.ds(pl.multiple_of(t * rows, 16), rows), :]

    for k in range(1, chan):
        rsend[k] = block_of(flip(z, k)).astype(BF)

    for group in range(1, groups):
        for k in range(group * per, (group + 1) * per):
            gathers[k].wait_recv()
            if k == chan - 2:
                for c in sums:
                    c.start()
            fill_source(k)
        share(group)
        if group < groups - 1:
            spread(group)
    if groups > 1:
        gather_up(0)

    r32[0:9 * pad, :] = jnp.dot(wf[...], x3[:, LANE:LANE + span], preferred_element_type=F32)
    if groups > 1:
        spread(groups - 1)

    def relay(a):
        for h in range(height):
            t32[a, pl.ds(h, pad, stride=height), :] = shifted(pad, a * pad, 3 * pad, h)

    stack[...] = jnp.zeros_like(stack)
    relay(0)
    psend[0] = t32[0, 0:rows, :].astype(BF)
    pair = (send(psend.at[0], precv.at[0], p_s.at[0], p_r.at[0], {"space": up}),
            send(psend.at[1], precv.at[1], p_s.at[1], p_r.at[1], {"space": down}))
    pl.when(has_up)(pair[0].start)
    relay(2)
    psend[1] = t32[2, 0:rows, :].astype(BF)
    pl.when(has_down)(pair[1].start)
    for k in range(1, groups - 1):
        gather_up(k)
    relay(1)

    for k in range(groups - 1):
        collect(k)
    gather_up(groups - 1)
    collect(groups - 1)
    for a in range(3):
        for b in range(3):
            for c in range(3):
                at = b * tall + a * some
                wg_ref[(a * 3 + b) * 3 + c] = (
                    acc[at:at + blk, c * wide:c * wide + channels] * scale)

    pl.when(has_down)(pair[0].wait_recv)
    pl.when(has_up)(pair[1].wait_recv)
    out_ref[...] = (t32[1, 0:rows, :] + precv[0].astype(F32)
                    + precv[1].astype(F32)).astype(BF)

    for c in sums:
        c.wait_recv()
    total = block_of(z)
    for k in range(1, chan):
        total = total + rrecv[k].astype(F32)
    back_ref[...] = total.astype(BF)

    for c in gathers[1:] + sums + pairs + passes:
        c.wait_send()
    for group in shares:
        for c in group:
            c.wait_send()
    for c in (halo_up, pair[0]):
        pl.when(has_up)(c.wait_send)
    for c in (halo_down, pair[1]):
        pl.when(has_down)(c.wait_send)


def write(*refs):
    n = len(refs) // 2
    copies = [pltpu.make_async_copy(refs[i], refs[n + i], refs[-1].at[i]) for i in range(n)]
    for c in copies:
        c.start()
    for c in copies:
        c.wait()


def body(space, chan, activation, weights, cotangent):
    planes, blk, height, width = activation.shape
    channels = weights.shape[3]
    assert planes == 1 and width == LANE
    pad = up_to(blk, 16)
    rows = blk * height
    groups = min(chan, 4)
    scale = 1.0 / math.sqrt(planes * space * height * width)
    dma = pltpu.SemaphoreType.DMA
    vm = pltpu.VMEM
    some = up_to(blk, 8)
    ring = up_to(3 * some, 16)
    deep = ring * chan
    per = chan // groups
    tall = ring
    half = up_to(3 * (3 * some if per == 1 else per * ring), 2 * LANE) // 2
    flat = up_to(per * ring, LANE)
    wide = up_to(channels, LANE)
    shapes = (
        jax.ShapeDtypeStruct((rows, LANE), BF),
        jax.ShapeDtypeStruct((rows, LANE), BF),
        jax.ShapeDtypeStruct((27, blk, channels), F32),
    )
    outs = pl.pallas_call(
        functools.partial(kernel, space, chan, blk, pad, channels, height, groups, scale),
        out_shape=shapes,
        in_specs=[pl.BlockSpec(memory_space=pltpu.HBM)] * 3,
        out_specs=[pl.BlockSpec(memory_space=vm)] * 3,
        scratch_shapes=[
            vm((chan, rows, LANE), BF),
            vm((rows, LANE), BF),
            vm((27, channels, channels), BF),
            vm((deep, (height + 2) * LANE), BF),
            vm((9 * pad, height * LANE), BF),
            vm((3, 9 * pad, channels), BF),
            vm((9 * pad, deep), BF),
            vm((3 * channels, 9 * pad), BF),
            vm((3, pad * height, LANE), F32),
            vm((3, pad * height, LANE), F32),
            vm((max(9 * pad, 3 * channels), height * LANE), F32),
            vm((channels * height, LANE), F32),
            vm((2, rows, LANE), BF),
            vm((2, rows, LANE), BF),
            vm((2, rows, LANE), BF),
            vm((groups, tall, 2 * half), F32),
            vm((groups, tall, half), BF),
            vm((groups, tall, half), BF),
            vm((groups, space, tall, half), BF),
            vm((groups, 2, tall, half), BF),
            vm((3 * tall, flat), BF),
            vm((3 * tall, 3 * wide), F32),
            vm((groups, flat, 3 * wide), BF),
            vm((chan, rows, LANE), BF),
            vm((chan, rows, LANE), BF),
            dma((3,)), dma((chan,)), dma((chan,)), dma((2,)), dma((2,)), dma((2,)), dma((2,)),
            dma((groups,)), dma((groups,)), dma((groups, space)), dma((groups, space)),
            dma((groups,)), dma((groups,)),
            dma((chan,)), dma((chan,)),
        ],
        compiler_params=pltpu.CompilerParams(
            collective_id=0, has_side_effects=True, vmem_limit_bytes=40 * 2**20),
    )(*[pltpu.with_memory_space_constraint(x, pltpu.HBM) for x in (
        activation.reshape(rows, width), cotangent.reshape(rows, width),
        weights.reshape(27, channels, channels))])
    out, back, grads = pl.pallas_call(
        write,
        out_shape=shapes,
        in_specs=[pl.BlockSpec(memory_space=vm)] * 3,
        out_specs=[pl.BlockSpec(memory_space=pltpu.HBM)] * 3,
        scratch_shapes=[dma((3,))],
        compiler_params=pltpu.CompilerParams(vmem_limit_bytes=2**20),
    )(*outs)
    field = (1, blk, height, width)
    grads = jnp.swapaxes(grads.reshape(3, 3, 3, blk, channels), 3, 4)
    return out.reshape(field), back.reshape(field), grads


def solution(mesh):
    field = P("space", "chan", None, None)
    return jax.shard_map(
        functools.partial(body, mesh.shape["space"], mesh.shape["chan"]),
        mesh=mesh,
        in_specs=(field, P(), field),
        out_specs=(field, field, P(None, None, None, None, "chan")),
        check_vma=False,
    )
```

```python
import functools
import math

import jax
import jax.numpy as jnp
from jax import lax
from jax.experimental import pallas as pl
from jax.experimental.pallas import tpu as pltpu
from jax.sharding import PartitionSpec as P

BF, F32 = jnp.bfloat16, jnp.float32
LANE = 128
ROWS_T = (((1,), (1,)), ((), ()))


def up_to(n, m):
    return -(-n // m) * m


def flip(i, m):
    out = i
    for b in range(m.bit_length()):
        if m >> b & 1:
            bit = lax.rem(lax.div(i, 1 << b), 2)
            out = out + (1 << b) * (1 - 2 * bit)
    return out


def kernel(space, chan, blk, pad, channels, height, groups, scale,
           a_hbm, g_hbm, w_hbm, out_ref, back_ref, wg_ref,
           ga, gv, w_ref, x3, xg, wt, wf, wb, z32, t32, r32, part,
           halo, psend, precv, wflat, csend, crecv, wall, full, stack, acc, place_q,
           nsend, nrecv, rsend, rrecv,
           l_s, g_s, g_r, h_s, h_r, p_s, p_r, c_s, c_r, w_s, w_r, f_s, f_r, n_s, n_r, r_s, r_r):
    e = lax.axis_index("space")
    z = lax.axis_index("chan")
    rows = blk * height
    span = height * LANE
    per = chan // groups
    tall, half = wall.shape[2], wall.shape[3]
    some = up_to(blk, 8)
    ring = up_to(3 * some, 16)
    each = 3 * some if per == 1 else per * ring
    wide = acc.shape[1] // 3
    up, down = lax.rem(e + 1, space), lax.rem(e + space - 1, space)
    core = lax.rem(e, 2)

    barrier = pltpu.get_barrier_semaphore()
    others = [{"chan": flip(z, k)} for k in range(1, chan)]
    others += [{"space": flip(e, k)} for k in range(1, space)]
    for other in others:
        pl.semaphore_signal(barrier, inc=1, device_id=other)
    loads = [pltpu.make_async_copy(a_hbm, ga.at[0], l_s.at[1]),
             pltpu.make_async_copy(g_hbm, gv, l_s.at[0]),
             pltpu.make_async_copy(w_hbm, w_ref, l_s.at[2])]
    for c in loads:
        c.start()

    def send(src, dst, ssem, rsem, to):
        return pltpu.make_async_remote_copy(src, dst, ssem, rsem, device_id=to)

    gathers = [None] + [
        send(ga.at[0], ga.at[k], g_s.at[k], g_r.at[k], {"chan": flip(z, k)})
        for k in range(1, chan)]
    halo_up = send(gv, halo.at[0], h_s.at[0], h_r.at[0], {"space": up})
    halo_down = send(gv, halo.at[1], h_s.at[1], h_r.at[1], {"space": down})
    has_up, has_down = e < space - 1, e > 0

    pl.semaphore_wait(barrier, len(others))
    loads[0].wait()
    for c in gathers[1:]:
        c.start()
    loads[1].wait()
    pl.when(has_up)(halo_up.start)
    pl.when(has_down)(halo_down.start)

    def no_lower():
        halo[0] = jnp.zeros((rows, LANE), BF)
        precv[0] = jnp.zeros((rows, LANE), BF)

    def no_upper():
        halo[1] = jnp.zeros((rows, LANE), BF)
        precv[1] = jnp.zeros((rows, LANE), BF)

    pl.when(e == 0)(no_lower)
    pl.when(e == space - 1)(no_upper)

    z32[...] = jnp.zeros_like(z32)
    x3[:, 0:LANE] = jnp.zeros((x3.shape[0], LANE), BF)
    x3[:, span + LANE:span + 2 * LANE] = jnp.zeros((x3.shape[0], LANE), BF)
    wflat[...] = jnp.zeros_like(wflat)
    stack[...] = jnp.zeros_like(stack)
    few = lax.broadcasted_iota(jnp.int32, (rows, LANE), 1)

    def shift(src):
        v = src.astype(F32)
        z32[0, 0:rows, :] = jnp.where(few == 0, 0.0, pltpu.roll(v, 1, 1))
        z32[1, 0:rows, :] = v
        z32[2, 0:rows, :] = jnp.where(few == LANE - 1, 0.0, pltpu.roll(v, LANE - 1, 1))

    def fill_signal(a, src):
        shift(src)
        for c in range(3):
            at = (c * 3 + a) * pad
            for h in range(height):
                xg[at:at + pad, h * LANE:(h + 1) * LANE] = (
                    z32[c, pl.ds(h, pad, stride=height), :].astype(BF))

    def fill_source(k):
        shift(ga[k])
        rest = [jnp.zeros((ring - 3 * some, LANE), F32)] if ring > 3 * some else []
        for h in range(height):
            taps = [z32[c, pl.ds(h, some, stride=height), :] for c in range(3)]
            x3[k * ring:(k + 1) * ring, (h + 1) * LANE:(h + 2) * LANE] = (
                jnp.concatenate(taps + rest, axis=0).astype(BF))

    fill_signal(1, gv[...])
    fill_source(0)

    loads[2].wait()
    thick = 9 * pad
    first = lax.broadcasted_iota(jnp.int32, (channels, thick), 0) - z * blk
    place = lax.broadcasted_iota(jnp.int32, (channels, thick), 1)
    inside = (first >= 0) & (first < blk)
    for b in range(3):
        total = jnp.zeros((channels, thick), F32)
        for c in range(3):
            for a in range(3):
                spot = inside & (place == first + (c * 3 + a) * pad)
                tap = w_ref[(a * 3 + 2 - b) * 3 + 2 - c]
                total = total + jnp.dot(
                    tap, jnp.where(spot, 1.0, 0.0).astype(BF), preferred_element_type=F32)
        wb[b * channels:(b + 1) * channels, :] = total.astype(BF)

    row = lax.broadcasted_iota(jnp.int32, (pad, channels), 0)
    col = lax.broadcasted_iota(jnp.int32, (pad, channels), 1)
    pick = jnp.where((col == row + z * blk) & (row < blk), 1.0, 0.0).astype(BF)
    for a in range(3):
        for b in range(3):
            for c in range(3):
                at = (b * 3 + a) * pad
                wt[c, at:at + pad, :] = lax.dot_general(
                    pick, w_ref[(a * 3 + b) * 3 + c], ROWS_T,
                    preferred_element_type=F32).astype(BF)
    deep = x3.shape[0]
    channel = lax.broadcasted_iota(jnp.int32, (channels, deep), 0)
    spot = lax.broadcasted_iota(jnp.int32, (channels, deep), 1)
    goes = jnp.zeros((channels, deep), jnp.int32)
    for k in range(chan):
        local = channel - flip(z, k) * blk
        goes = jnp.where((local >= 0) & (local < blk), local + k * ring, goes)
    total = jnp.zeros((9 * pad, deep), F32)
    for c in range(3):
        total = total + jnp.dot(
            wt[c], jnp.where(spot == goes + c * some, 1.0, 0.0).astype(BF),
            preferred_element_type=F32)
    wf[...] = total.astype(BF)

    place_q[...] = jnp.zeros_like(place_q)
    row = lax.broadcasted_iota(jnp.int32, (ring, wide), 0)
    col = lax.broadcasted_iota(jnp.int32, (ring, wide), 1)
    for k in range(chan):
        at = (k % per) * ring
        for c in range(3):
            own = row - c * some
            hit = (own >= 0) & (own < blk) & (col == own + flip(z, k) * blk)
            place_q[k // per, at:at + ring, c * wide:(c + 1) * wide] = (
                jnp.where(hit, 1.0, 0.0).astype(BF))

    pairs = [send(csend.at[k], crecv.at[k], c_s.at[k], c_r.at[k], {"space": flip(e, 1)})
             for k in range(groups)]
    shares = [[send(wall.at[k, e], wall.at[k, e], w_s.at[k, m], w_r.at[k, m],
                    {"space": flip(e, m)})
               for m in reversed(range(2, space, 2))]
              for k in range(groups)]
    passes = [send(full.at[k, core], full.at[k, core], f_s.at[k], f_r.at[k],
                   {"space": flip(e, 1)}) for k in range(groups)]

    def my_half(k, which):
        return wflat[k, :, pl.ds(pl.multiple_of(which * half, LANE), half)]

    def share(k):
        many = per * ring
        for b in range(3):
            one = lax.dot_general(
                xg[3 * pad:6 * pad, :],
                x3[k * many:(k + 1) * many, b * LANE:b * LANE + span],
                ROWS_T, preferred_element_type=F32)
            for a in range(3):
                wflat[k, a * some:(a + 1) * some, b * each:(b + 1) * each] = (
                    one[a * pad:a * pad + some, 0:each])
        csend[k] = my_half(k, 1 - core).astype(BF)
        pairs[k].start()

    def spread(k):
        pairs[k].wait_recv()
        wall[k, e] = (my_half(k, core) + crecv[k].astype(F32)).astype(BF)
        for c in shares[k]:
            c.start()

    def summed(k, side):
        total = wall[k, side].astype(F32)
        for chip in range(1, space // 2):
            total = total + wall[k, 2 * chip + side].astype(F32)
        return total.astype(BF)

    def gather_up(k):
        for c in shares[k]:
            c.wait_recv()
        full[k, core] = summed(k, core)
        passes[k].start()

    def collect(k):
        passes[k].wait_recv()
        both = jnp.concatenate([full[k, 0], full[k, 1]], axis=1)
        for b in range(3):
            stack[b * tall:(b + 1) * tall, 0:each] = both[:, b * each:(b + 1) * each]
        moved = jnp.dot(stack[...], place_q[k], preferred_element_type=F32)
        acc[...] = moved if k == 0 else acc[...] + moved

    pl.when(has_down)(halo_up.wait_recv)
    fill_signal(2, halo[0])
    pl.when(has_up)(halo_down.wait_recv)
    fill_signal(0, halo[1])
    for k in range(1, per):
        gathers[k].wait_recv()
        fill_source(k)
    share(0)

    def shifted(count, first_row, group, h):
        def piece(b, hh):
            at = first_row + b * group
            return r32[at:at + count, hh * LANE:(hh + 1) * LANE]
        v = piece(1, h)
        if h > 0:
            v = v + piece(0, h - 1)
        if h < height - 1:
            v = v + piece(2, h + 1)
        return v

    r32[0:3 * channels, :] = jnp.dot(wb[...], xg[...], preferred_element_type=F32)
    spread(0)
    for h in range(height):
        part[pl.ds(h, channels, stride=height), :] = shifted(channels, 0, channels, h)

    near = [send(nsend.at[k], nrecv.at[k], n_s.at[k], n_r.at[k], {"chan": flip(z, 1)})
            for k in range(chan // 2)]
    sums = [send(rsend.at[k], rrecv.at[k], r_s.at[k], r_r.at[k], {"chan": flip(z, 2 * k)})
            for k in range(1, chan // 2)]

    def block_of(t):
        return part[pl.ds(pl.multiple_of(t * rows, 16), rows), :]

    for k in reversed(range(chan // 2)):
        nsend[k] = block_of(flip(z, 2 * k + 1)).astype(BF)
    for c in near[1:]:
        c.start()

    def pass_on():
        for k in range(1, chan // 2):
            near[k].wait_recv()
            rsend[k] = (block_of(flip(z, 2 * k)) + nrecv[k].astype(F32)).astype(BF)
            sums[k - 1].start()

    for group in range(1, groups):
        for k in range(group * per, (group + 1) * per):
            gathers[k].wait_recv()
            if k == chan - 1:
                near[0].start()
            fill_source(k)
        share(group)
        if group == 1 and groups > 2:
            spread(1)
        elif group > 2:
            spread(group - 1)

    pass_on()
    if groups > 1:
        spread(groups - 1)
    r32[0:9 * pad, :] = jnp.dot(wf[...], x3[:, LANE:LANE + span], preferred_element_type=F32)

    def relay(a):
        for h in range(height):
            t32[a, pl.ds(h, pad, stride=height), :] = shifted(pad, a * pad, 3 * pad, h)

    relay(0)
    psend[0] = t32[0, 0:rows, :].astype(BF)
    pair = (send(psend.at[0], precv.at[0], p_s.at[0], p_r.at[0], {"space": up}),
            send(psend.at[1], precv.at[1], p_s.at[1], p_r.at[1], {"space": down}))
    pl.when(has_up)(pair[0].start)
    relay(2)
    psend[1] = t32[2, 0:rows, :].astype(BF)
    pl.when(has_down)(pair[1].start)
    for k in range(groups - 1):
        gather_up(k)
    relay(1)

    for k in range(groups - 1):
        collect(k)
    gather_up(groups - 1)
    collect(groups - 1)
    for a in range(3):
        for b in range(3):
            for c in range(3):
                at = b * tall + a * some
                wg_ref[(a * 3 + b) * 3 + c] = (
                    acc[at:at + blk, c * wide:c * wide + channels] * scale)

    pl.when(has_down)(pair[0].wait_recv)
    pl.when(has_up)(pair[1].wait_recv)
    out_ref[...] = (t32[1, 0:rows, :] + precv[0].astype(F32)
                    + precv[1].astype(F32)).astype(BF)

    for c in sums:
        c.wait_recv()
    near[0].wait_recv()
    total = block_of(z) + nrecv[0].astype(F32)
    for k in range(1, chan // 2):
        total = total + rrecv[k].astype(F32)
    back_ref[...] = total.astype(BF)

    for c in gathers[1:] + near + sums + pairs + passes:
        c.wait_send()
    for group in shares:
        for c in group:
            c.wait_send()
    for c in (halo_up, pair[0]):
        pl.when(has_up)(c.wait_send)
    for c in (halo_down, pair[1]):
        pl.when(has_down)(c.wait_send)


def write(*refs):
    n = len(refs) // 2
    copies = [pltpu.make_async_copy(refs[i], refs[n + i], refs[-1].at[i]) for i in range(n)]
    for c in copies:
        c.start()
    for c in copies:
        c.wait()


def body(space, chan, activation, weights, cotangent):
    planes, blk, height, width = activation.shape
    channels = weights.shape[3]
    assert planes == 1 and width == LANE
    pad = up_to(blk, 16)
    rows = blk * height
    groups = min(chan, 4)
    scale = 1.0 / math.sqrt(planes * space * height * width)
    dma = pltpu.SemaphoreType.DMA
    vm = pltpu.VMEM
    some = up_to(blk, 8)
    ring = up_to(3 * some, 16)
    deep = ring * chan
    per = chan // groups
    tall = ring
    half = up_to(3 * (3 * some if per == 1 else per * ring), 2 * LANE) // 2
    flat = up_to(per * ring, LANE)
    wide = up_to(channels, LANE)
    shapes = (
        jax.ShapeDtypeStruct((rows, LANE), BF),
        jax.ShapeDtypeStruct((rows, LANE), BF),
        jax.ShapeDtypeStruct((27, blk, channels), F32),
    )
    outs = pl.pallas_call(
        functools.partial(kernel, space, chan, blk, pad, channels, height, groups, scale),
        out_shape=shapes,
        in_specs=[pl.BlockSpec(memory_space=pltpu.HBM)] * 3,
        out_specs=[pl.BlockSpec(memory_space=vm)] * 3,
        scratch_shapes=[
            vm((chan, rows, LANE), BF),
            vm((rows, LANE), BF),
            vm((27, channels, channels), BF),
            vm((deep, (height + 2) * LANE), BF),
            vm((9 * pad, height * LANE), BF),
            vm((3, 9 * pad, channels), BF),
            vm((9 * pad, deep), BF),
            vm((3 * channels, 9 * pad), BF),
            vm((3, pad * height, LANE), F32),
            vm((3, pad * height, LANE), F32),
            vm((max(9 * pad, 3 * channels), height * LANE), F32),
            vm((channels * height, LANE), F32),
            vm((2, rows, LANE), BF),
            vm((2, rows, LANE), BF),
            vm((2, rows, LANE), BF),
            vm((groups, tall, 2 * half), F32),
            vm((groups, tall, half), BF),
            vm((groups, tall, half), BF),
            vm((groups, space, tall, half), BF),
            vm((groups, 2, tall, half), BF),
            vm((3 * tall, flat), BF),
            vm((3 * tall, 3 * wide), F32),
            vm((groups, flat, 3 * wide), BF),
            vm((chan // 2, rows, LANE), BF),
            vm((chan // 2, rows, LANE), BF),
            vm((chan // 2, rows, LANE), BF),
            vm((chan // 2, rows, LANE), BF),
            dma((3,)), dma((chan,)), dma((chan,)), dma((2,)), dma((2,)), dma((2,)), dma((2,)),
            dma((groups,)), dma((groups,)), dma((groups, space)), dma((groups, space)),
            dma((groups,)), dma((groups,)),
            dma((chan // 2,)), dma((chan // 2,)), dma((chan // 2,)), dma((chan // 2,)),
        ],
        compiler_params=pltpu.CompilerParams(
            collective_id=0, has_side_effects=True, vmem_limit_bytes=40 * 2**20),
    )(*[pltpu.with_memory_space_constraint(x, pltpu.HBM) for x in (
        activation.reshape(rows, width), cotangent.reshape(rows, width),
        weights.reshape(27, channels, channels))])
    out, back, grads = pl.pallas_call(
        write,
        out_shape=shapes,
        in_specs=[pl.BlockSpec(memory_space=vm)] * 3,
        out_specs=[pl.BlockSpec(memory_space=pltpu.HBM)] * 3,
        scratch_shapes=[dma((3,))],
        compiler_params=pltpu.CompilerParams(vmem_limit_bytes=2**20),
    )(*outs)
    field = (1, blk, height, width)
    grads = jnp.swapaxes(grads.reshape(3, 3, 3, blk, channels), 3, 4)
    return out.reshape(field), back.reshape(field), grads


def solution(mesh):
    field = P("space", "chan", None, None)
    return jax.shard_map(
        functools.partial(body, mesh.shape["space"], mesh.shape["chan"]),
        mesh=mesh,
        in_specs=(field, P(), field),
        out_specs=(field, field, P(None, None, None, None, "chan")),
        check_vma=False,
    )
```

```python
import functools
import math

import jax
import jax.numpy as jnp
from jax import lax
from jax.experimental import pallas as pl
from jax.experimental.pallas import tpu as pltpu
from jax.sharding import PartitionSpec as P

BF, F32 = jnp.bfloat16, jnp.float32
LANE = 128
ROWS_T = (((1,), (1,)), ((), ()))


def up_to(n, m):
    return -(-n // m) * m


def flip(i, m):
    out = i
    for b in range(m.bit_length()):
        if m >> b & 1:
            bit = lax.rem(lax.div(i, 1 << b), 2)
            out = out + (1 << b) * (1 - 2 * bit)
    return out


def kernel(space, chan, blk, pad, channels, height, cuts, scale,
           a_hbm, g_hbm, w_hbm, out_ref, back_ref, wg_ref,
           ga, gv, w_ref, x3, xg, wt, wf, wb, z32, t32, r32, part,
           halo, psend, precv, wflat, csend, crecv, wall, full, stack, acc, place_q,
           nsend, nrecv, rsend, rrecv,
           l_s, g_s, g_r, h_s, h_r, p_s, p_r, c_s, c_r, w_s, w_r, f_s, f_r, n_s, n_r, r_s, r_r):
    e = lax.axis_index("space")
    z = lax.axis_index("chan")
    rows = blk * height
    span = height * LANE
    groups = len(cuts)
    begin = [sum(cuts[:g]) for g in range(groups + 1)]
    tall = full[0].shape[1]
    some = up_to(blk, 8)
    ring = up_to(3 * some, 16)
    each = [n * ring for n in cuts]
    wide = acc.shape[1] // 3
    up, down = lax.rem(e + 1, space), lax.rem(e + space - 1, space)
    core = lax.rem(e, 2)

    barrier = pltpu.get_barrier_semaphore()
    others = [{"chan": flip(z, k)} for k in range(1, chan)]
    others += [{"space": flip(e, k)} for k in range(1, space)]
    for other in others:
        pl.semaphore_signal(barrier, inc=1, device_id=other)
    loads = [pltpu.make_async_copy(a_hbm, ga.at[0], l_s.at[1]),
             pltpu.make_async_copy(g_hbm, gv, l_s.at[0]),
             pltpu.make_async_copy(w_hbm, w_ref, l_s.at[2])]
    for c in loads:
        c.start()

    def send(src, dst, ssem, rsem, to):
        return pltpu.make_async_remote_copy(src, dst, ssem, rsem, device_id=to)

    gathers = [None] + [
        send(ga.at[0], ga.at[k], g_s.at[k], g_r.at[k], {"chan": flip(z, k)})
        for k in range(1, chan)]
    halo_up = send(gv, halo.at[0], h_s.at[0], h_r.at[0], {"space": up})
    halo_down = send(gv, halo.at[1], h_s.at[1], h_r.at[1], {"space": down})
    has_up, has_down = e < space - 1, e > 0

    pl.semaphore_wait(barrier, len(others))
    loads[0].wait()
    for c in gathers[1:]:
        c.start()
    loads[1].wait()
    pl.when(has_up)(halo_up.start)
    pl.when(has_down)(halo_down.start)

    def no_lower():
        halo[0] = jnp.zeros((rows, LANE), BF)
        precv[0] = jnp.zeros((rows, LANE), BF)

    def no_upper():
        halo[1] = jnp.zeros((rows, LANE), BF)
        precv[1] = jnp.zeros((rows, LANE), BF)

    pl.when(e == 0)(no_lower)
    pl.when(e == space - 1)(no_upper)

    z32[...] = jnp.zeros_like(z32)
    x3[:, 0:LANE] = jnp.zeros((x3.shape[0], LANE), BF)
    x3[:, span + LANE:span + 2 * LANE] = jnp.zeros((x3.shape[0], LANE), BF)
    for ref in (*wflat, *stack, *place_q):
        ref[...] = jnp.zeros_like(ref)
    few = lax.broadcasted_iota(jnp.int32, (rows, LANE), 1)

    def shift(src):
        v = src.astype(F32)
        z32[0, 0:rows, :] = jnp.where(few == 0, 0.0, pltpu.roll(v, 1, 1))
        z32[1, 0:rows, :] = v
        z32[2, 0:rows, :] = jnp.where(few == LANE - 1, 0.0, pltpu.roll(v, LANE - 1, 1))

    def fill_signal(a, src):
        shift(src)
        for c in range(3):
            at = (c * 3 + a) * pad
            for h in range(height):
                xg[at:at + pad, h * LANE:(h + 1) * LANE] = (
                    z32[c, pl.ds(h, pad, stride=height), :].astype(BF))

    def fill_source(k):
        shift(ga[k])
        rest = [jnp.zeros((ring - 3 * some, LANE), F32)] if ring > 3 * some else []
        for h in range(height):
            taps = [z32[c, pl.ds(h, some, stride=height), :] for c in range(3)]
            x3[k * ring:(k + 1) * ring, (h + 1) * LANE:(h + 2) * LANE] = (
                jnp.concatenate(taps + rest, axis=0).astype(BF))

    fill_signal(1, gv[...])
    fill_source(0)

    loads[2].wait()
    thick = 9 * pad
    first = lax.broadcasted_iota(jnp.int32, (channels, thick), 0) - z * blk
    place = lax.broadcasted_iota(jnp.int32, (channels, thick), 1)
    inside = (first >= 0) & (first < blk)
    for b in range(3):
        total = jnp.zeros((channels, thick), F32)
        for c in range(3):
            for a in range(3):
                spot = inside & (place == first + (c * 3 + a) * pad)
                tap = w_ref[(a * 3 + 2 - b) * 3 + 2 - c]
                total = total + jnp.dot(
                    tap, jnp.where(spot, 1.0, 0.0).astype(BF), preferred_element_type=F32)
        wb[b * channels:(b + 1) * channels, :] = total.astype(BF)

    row = lax.broadcasted_iota(jnp.int32, (pad, channels), 0)
    col = lax.broadcasted_iota(jnp.int32, (pad, channels), 1)
    pick = jnp.where((col == row + z * blk) & (row < blk), 1.0, 0.0).astype(BF)
    for a in range(3):
        for b in range(3):
            for c in range(3):
                at = (b * 3 + a) * pad
                wt[c, at:at + pad, :] = lax.dot_general(
                    pick, w_ref[(a * 3 + b) * 3 + c], ROWS_T,
                    preferred_element_type=F32).astype(BF)
    deep = x3.shape[0]
    channel = lax.broadcasted_iota(jnp.int32, (channels, deep), 0)
    spot = lax.broadcasted_iota(jnp.int32, (channels, deep), 1)
    goes = jnp.zeros((channels, deep), jnp.int32)
    for k in range(chan):
        local = channel - flip(z, k) * blk
        goes = jnp.where((local >= 0) & (local < blk), local + k * ring, goes)
    total = jnp.zeros((9 * pad, deep), F32)
    for c in range(3):
        total = total + jnp.dot(
            wt[c], jnp.where(spot == goes + c * some, 1.0, 0.0).astype(BF),
            preferred_element_type=F32)
    wf[...] = total.astype(BF)

    row = lax.broadcasted_iota(jnp.int32, (ring, wide), 0)
    col = lax.broadcasted_iota(jnp.int32, (ring, wide), 1)
    for g in range(groups):
        for k in range(begin[g], begin[g + 1]):
            at = (k - begin[g]) * ring
            for c in range(3):
                own = row - c * some
                hit = (own >= 0) & (own < blk) & (col == own + flip(z, k) * blk)
                place_q[g][at:at + ring, c * wide:(c + 1) * wide] = (
                    jnp.where(hit, 1.0, 0.0).astype(BF))

    last = groups - 1
    pairs = [send(csend[g], crecv[g], c_s.at[g], c_r.at[g], {"space": flip(e, 1)})
             for g in range(last)]

    def reach(g):
        return range(1 if g == last else 2, space, 1 if g == last else 2)

    def piece_of(g, m):
        return csend[g] if m % 2 else wall[g].at[e]

    shares = [[send(piece_of(g, m), wall[g].at[e], w_s.at[g, m], w_r.at[g, m],
                    {"space": flip(e, m)}) for m in reversed(reach(g))]
              for g in range(groups)]
    passes = [send(full[g].at[core], full[g].at[core], f_s.at[g], f_r.at[g],
                   {"space": flip(e, 1)}) for g in range(groups)]

    def my_half(g, which):
        half = full[g].shape[2]
        return wflat[g][:, pl.ds(pl.multiple_of(which * half, LANE), half)]

    def share(g):
        for b in range(3):
            one = lax.dot_general(
                xg[3 * pad:6 * pad, :],
                x3[begin[g] * ring:begin[g + 1] * ring, b * LANE:b * LANE + span],
                ROWS_T, preferred_element_type=F32)
            for a in range(3):
                wflat[g][a * some:(a + 1) * some, b * each[g]:(b + 1) * each[g]] = (
                    one[a * pad:a * pad + some, :])
        csend[g][...] = my_half(g, 1 - core).astype(BF)
        if g == last:
            wall[g][e] = my_half(g, core).astype(BF)
            for c in shares[g]:
                c.start()
        else:
            pairs[g].start()

    def spread(g):
        if g == last:
            return
        pairs[g].wait_recv()
        wall[g][e] = (my_half(g, core) + crecv[g][...].astype(F32)).astype(BF)
        for c in shares[g]:
            c.start()

    def gather_up(g):
        for c in shares[g]:
            c.wait_recv()
        if g == last:
            total = wall[g][0].astype(F32)
            for origin in range(1, space):
                total = total + wall[g][origin].astype(F32)
        else:
            total = wall[g][core].astype(F32)
            for chip in range(1, space // 2):
                total = total + wall[g][2 * chip + core].astype(F32)
        full[g][core] = total.astype(BF)
        passes[g].start()

    def collect(g):
        passes[g].wait_recv()
        both = jnp.concatenate([full[g][0], full[g][1]], axis=1)
        for b in range(3):
            stack[g][b * tall:(b + 1) * tall, 0:each[g]] = both[:, b * each[g]:(b + 1) * each[g]]
        moved = jnp.dot(stack[g][...], place_q[g][...], preferred_element_type=F32)
        acc[...] = moved if g == 0 else acc[...] + moved

    pl.when(has_down)(halo_up.wait_recv)
    fill_signal(2, halo[0])
    pl.when(has_up)(halo_down.wait_recv)
    fill_signal(0, halo[1])

    def shifted(count, first_row, group, h):
        def piece(b, hh):
            at = first_row + b * group
            return r32[at:at + count, hh * LANE:(hh + 1) * LANE]
        v = piece(1, h)
        if h > 0:
            v = v + piece(0, h - 1)
        if h < height - 1:
            v = v + piece(2, h + 1)
        return v

    r32[0:3 * channels, :] = jnp.dot(wb[...], xg[...], preferred_element_type=F32)
    for h in range(height):
        part[pl.ds(h, channels, stride=height), :] = shifted(channels, 0, channels, h)

    near = [send(nsend.at[k], nrecv.at[k], n_s.at[k], n_r.at[k], {"chan": flip(z, 1)})
            for k in range(chan // 2)]
    sums = [send(rsend.at[k], rrecv.at[k], r_s.at[k], r_r.at[k], {"chan": flip(z, 2 * k)})
            for k in range(1, chan // 2)]

    def block_of(t):
        return part[pl.ds(pl.multiple_of(t * rows, 16), rows), :]

    for k in reversed(range(chan // 2)):
        nsend[k] = block_of(flip(z, 2 * k + 1)).astype(BF)
    for c in near[1:]:
        c.start()

    def pass_on():
        for k in range(1, chan // 2):
            near[k].wait_recv()
            rsend[k] = (block_of(flip(z, 2 * k)) + nrecv[k].astype(F32)).astype(BF)
            sums[k - 1].start()

    for g in range(groups):
        for k in range(max(begin[g], 1), begin[g + 1]):
            gathers[k].wait_recv()
            if k == chan - 1:
                near[0].start()
            fill_source(k)
        share(g)
        if g < groups - 1:
            spread(g)

    pass_on()
    spread(groups - 1)
    r32[0:9 * pad, :] = jnp.dot(wf[...], x3[:, LANE:LANE + span], preferred_element_type=F32)

    def relay(a):
        for h in range(height):
            t32[a, pl.ds(h, pad, stride=height), :] = shifted(pad, a * pad, 3 * pad, h)

    relay(0)
    psend[0] = t32[0, 0:rows, :].astype(BF)
    pair = (send(psend.at[0], precv.at[0], p_s.at[0], p_r.at[0], {"space": up}),
            send(psend.at[1], precv.at[1], p_s.at[1], p_r.at[1], {"space": down}))
    pl.when(has_up)(pair[0].start)
    relay(2)
    psend[1] = t32[2, 0:rows, :].astype(BF)
    pl.when(has_down)(pair[1].start)
    for k in range(groups - 1):
        gather_up(k)
    relay(1)

    for k in range(groups - 1):
        collect(k)
    gather_up(groups - 1)
    pl.when(has_down)(pair[0].wait_recv)
    pl.when(has_up)(pair[1].wait_recv)
    out_ref[...] = (t32[1, 0:rows, :] + precv[0].astype(F32)
                    + precv[1].astype(F32)).astype(BF)

    collect(groups - 1)
    for a in range(3):
        for b in range(3):
            for c in range(3):
                at = b * tall + a * some
                wg_ref[(a * 3 + b) * 3 + c] = (
                    acc[at:at + blk, c * wide:c * wide + channels] * scale)

    for c in sums:
        c.wait_recv()
    near[0].wait_recv()
    total = block_of(z) + nrecv[0].astype(F32)
    for k in range(1, chan // 2):
        total = total + rrecv[k].astype(F32)
    back_ref[...] = total.astype(BF)

    for c in gathers[1:] + near + sums + pairs + passes:
        c.wait_send()
    for group in shares:
        for c in group:
            c.wait_send()
    for c in (halo_up, pair[0]):
        pl.when(has_up)(c.wait_send)
    for c in (halo_down, pair[1]):
        pl.when(has_down)(c.wait_send)


def write(*refs):
    n = len(refs) // 2
    copies = [pltpu.make_async_copy(refs[i], refs[n + i], refs[-1].at[i]) for i in range(n)]
    for c in copies:
        c.start()
    for c in copies:
        c.wait()


def body(space, chan, activation, weights, cotangent):
    planes, blk, height, width = activation.shape
    channels = weights.shape[3]
    assert planes == 1 and width == LANE
    pad = up_to(blk, 16)
    rows = blk * height
    cuts = [chan // 2, chan // 4, chan // 4]
    scale = 1.0 / math.sqrt(planes * space * height * width)
    dma = pltpu.SemaphoreType.DMA
    vm = pltpu.VMEM
    some = up_to(blk, 8)
    ring = up_to(3 * some, 16)
    deep = ring * chan
    tall = ring
    flats = [up_to(n * ring, LANE) for n in cuts]
    halves = [up_to(3 * n * ring, 2 * LANE) // 2 for n in cuts]
    groups = len(cuts)
    wide = up_to(channels, LANE)
    shapes = (
        jax.ShapeDtypeStruct((rows, LANE), BF),
        jax.ShapeDtypeStruct((rows, LANE), BF),
        jax.ShapeDtypeStruct((27, blk, channels), F32),
    )
    outs = pl.pallas_call(
        functools.partial(kernel, space, chan, blk, pad, channels, height, cuts, scale),
        out_shape=shapes,
        in_specs=[pl.BlockSpec(memory_space=pltpu.HBM)] * 3,
        out_specs=[pl.BlockSpec(memory_space=vm)] * 3,
        scratch_shapes=[
            vm((chan, rows, LANE), BF),
            vm((rows, LANE), BF),
            vm((27, channels, channels), BF),
            vm((deep, (height + 2) * LANE), BF),
            vm((9 * pad, height * LANE), BF),
            vm((3, 9 * pad, channels), BF),
            vm((9 * pad, deep), BF),
            vm((3 * channels, 9 * pad), BF),
            vm((3, pad * height, LANE), F32),
            vm((3, pad * height, LANE), F32),
            vm((max(9 * pad, 3 * channels), height * LANE), F32),
            vm((channels * height, LANE), F32),
            vm((2, rows, LANE), BF),
            vm((2, rows, LANE), BF),
            vm((2, rows, LANE), BF),
            tuple(vm((tall, 2 * half), F32) for half in halves),
            tuple(vm((tall, half), BF) for half in halves),
            tuple(vm((tall, half), BF) for half in halves),
            tuple(vm((space, tall, half), BF) for half in halves),
            tuple(vm((2, tall, half), BF) for half in halves),
            tuple(vm((3 * tall, flat), BF) for flat in flats),
            vm((3 * tall, 3 * wide), F32),
            tuple(vm((flat, 3 * wide), BF) for flat in flats),
            vm((chan // 2, rows, LANE), BF),
            vm((chan // 2, rows, LANE), BF),
            vm((chan // 2, rows, LANE), BF),
            vm((chan // 2, rows, LANE), BF),
            dma((3,)), dma((chan,)), dma((chan,)), dma((2,)), dma((2,)), dma((2,)), dma((2,)),
            dma((groups,)), dma((groups,)), dma((groups, space)), dma((groups, space)),
            dma((groups,)), dma((groups,)),
            dma((chan // 2,)), dma((chan // 2,)), dma((chan // 2,)), dma((chan // 2,)),
        ],
        compiler_params=pltpu.CompilerParams(
            collective_id=0, has_side_effects=True, vmem_limit_bytes=40 * 2**20),
    )(*[pltpu.with_memory_space_constraint(x, pltpu.HBM) for x in (
        activation.reshape(rows, width), cotangent.reshape(rows, width),
        weights.reshape(27, channels, channels))])
    out, back, grads = pl.pallas_call(
        write,
        out_shape=shapes,
        in_specs=[pl.BlockSpec(memory_space=vm)] * 3,
        out_specs=[pl.BlockSpec(memory_space=pltpu.HBM)] * 3,
        scratch_shapes=[dma((3,))],
        compiler_params=pltpu.CompilerParams(vmem_limit_bytes=2**20),
    )(*outs)
    field = (1, blk, height, width)
    grads = jnp.swapaxes(grads.reshape(3, 3, 3, blk, channels), 3, 4)
    return out.reshape(field), back.reshape(field), grads


def solution(mesh):
    field = P("space", "chan", None, None)
    return jax.shard_map(
        functools.partial(body, mesh.shape["space"], mesh.shape["chan"]),
        mesh=mesh,
        in_specs=(field, P(), field),
        out_specs=(field, field, P(None, None, None, None, "chan")),
        check_vma=False,
    )
```

```python
import functools
import math

import jax
import jax.numpy as jnp
from jax import lax
from jax.experimental import pallas as pl
from jax.experimental.pallas import tpu as pltpu
from jax.sharding import PartitionSpec as P

BF, F32 = jnp.bfloat16, jnp.float32
LANE = 128
ROWS_T = (((1,), (1,)), ((), ()))


def up_to(n, m):
    return -(-n // m) * m


def flip(i, m):
    out = i
    for b in range(m.bit_length()):
        if m >> b & 1:
            bit = lax.rem(lax.div(i, 1 << b), 2)
            out = out + (1 << b) * (1 - 2 * bit)
    return out


def kernel(space, chan, blk, pad, channels, height, cuts, scale,
           a_hbm, g_hbm, w_hbm, out_ref, back_ref, wg_ref,
           ga, gv, w_ref, x3, xg, wt, wf, wb, z32, t32, r32, part,
           halo, psend, precv, wflat, csend, crecv, wall, full, stack, acc, place_q,
           nsend, nrecv, rsend, rrecv,
           l_s, g_s, g_r, h_s, h_r, p_s, p_r, c_s, c_r, w_s, w_r, f_s, f_r, n_s, n_r, r_s, r_r):
    e = lax.axis_index("space")
    z = lax.axis_index("chan")
    rows = blk * height
    span = height * LANE
    groups = len(cuts)
    begin = [sum(cuts[:g]) for g in range(groups + 1)]
    tall = full[0].shape[1]
    some = up_to(blk, 8)
    ring = up_to(3 * some, 16)
    each = [n * ring for n in cuts]
    wide = acc.shape[1] // 3
    up, down = lax.rem(e + 1, space), lax.rem(e + space - 1, space)
    core = lax.rem(e, 2)

    barrier = pltpu.get_barrier_semaphore()
    others = [{"chan": flip(z, k)} for k in range(1, chan)]
    others += [{"space": flip(e, k)} for k in range(1, space)]
    for other in others:
        pl.semaphore_signal(barrier, inc=1, device_id=other)
    loads = [pltpu.make_async_copy(a_hbm, ga.at[0], l_s.at[1]),
             pltpu.make_async_copy(g_hbm, gv, l_s.at[0]),
             pltpu.make_async_copy(w_hbm, w_ref, l_s.at[2])]
    for c in loads:
        c.start()

    def send(src, dst, ssem, rsem, to):
        return pltpu.make_async_remote_copy(src, dst, ssem, rsem, device_id=to)

    gathers = [None] + [
        send(ga.at[0], ga.at[k], g_s.at[k], g_r.at[k], {"chan": flip(z, k)})
        for k in range(1, chan)]
    halo_up = send(gv, halo.at[0], h_s.at[0], h_r.at[0], {"space": up})
    halo_down = send(gv, halo.at[1], h_s.at[1], h_r.at[1], {"space": down})
    has_up, has_down = e < space - 1, e > 0

    pl.semaphore_wait(barrier, len(others))
    loads[0].wait()
    for c in gathers[1:]:
        c.start()
    loads[1].wait()
    pl.when(has_up)(halo_up.start)
    pl.when(has_down)(halo_down.start)

    def no_lower():
        halo[0] = jnp.zeros((rows, LANE), BF)
        precv[0] = jnp.zeros((rows, LANE), BF)

    def no_upper():
        halo[1] = jnp.zeros((rows, LANE), BF)
        precv[1] = jnp.zeros((rows, LANE), BF)

    pl.when(e == 0)(no_lower)
    pl.when(e == space - 1)(no_upper)

    z32[...] = jnp.zeros_like(z32)
    x3[:, 0:LANE] = jnp.zeros((x3.shape[0], LANE), BF)
    x3[:, span + LANE:span + 2 * LANE] = jnp.zeros((x3.shape[0], LANE), BF)
    for ref in (*wflat, *stack, *place_q):
        ref[...] = jnp.zeros_like(ref)
    few = lax.broadcasted_iota(jnp.int32, (rows, LANE), 1)

    def shift(src):
        v = src.astype(F32)
        z32[0, 0:rows, :] = jnp.where(few == 0, 0.0, pltpu.roll(v, 1, 1))
        z32[1, 0:rows, :] = v
        z32[2, 0:rows, :] = jnp.where(few == LANE - 1, 0.0, pltpu.roll(v, LANE - 1, 1))

    def fill_signal(a, src):
        shift(src)
        for c in range(3):
            at = (c * 3 + a) * pad
            for h in range(height):
                xg[at:at + pad, h * LANE:(h + 1) * LANE] = (
                    z32[c, pl.ds(h, pad, stride=height), :].astype(BF))

    def fill_source(k):
        shift(ga[k])
        rest = [jnp.zeros((ring - 3 * some, LANE), F32)] if ring > 3 * some else []
        for h in range(height):
            taps = [z32[c, pl.ds(h, some, stride=height), :] for c in range(3)]
            x3[k * ring:(k + 1) * ring, (h + 1) * LANE:(h + 2) * LANE] = (
                jnp.concatenate(taps + rest, axis=0).astype(BF))

    fill_signal(1, gv[...])
    fill_source(0)

    loads[2].wait()
    thick = 9 * pad
    first = lax.broadcasted_iota(jnp.int32, (channels, thick), 0) - z * blk
    place = lax.broadcasted_iota(jnp.int32, (channels, thick), 1)
    inside = (first >= 0) & (first < blk)
    for b in range(3):
        total = jnp.zeros((channels, thick), F32)
        for c in range(3):
            for a in range(3):
                spot = inside & (place == first + (c * 3 + a) * pad)
                tap = w_ref[(a * 3 + 2 - b) * 3 + 2 - c]
                total = total + jnp.dot(
                    tap, jnp.where(spot, 1.0, 0.0).astype(BF), preferred_element_type=F32)
        wb[b * channels:(b + 1) * channels, :] = total.astype(BF)

    row = lax.broadcasted_iota(jnp.int32, (pad, channels), 0)
    col = lax.broadcasted_iota(jnp.int32, (pad, channels), 1)
    pick = jnp.where((col == row + z * blk) & (row < blk), 1.0, 0.0).astype(BF)
    for a in range(3):
        for b in range(3):
            for c in range(3):
                at = (b * 3 + a) * pad
                wt[c, at:at + pad, :] = lax.dot_general(
                    pick, w_ref[(a * 3 + b) * 3 + c], ROWS_T,
                    preferred_element_type=F32).astype(BF)
    deep = x3.shape[0]
    channel = lax.broadcasted_iota(jnp.int32, (channels, deep), 0)
    spot = lax.broadcasted_iota(jnp.int32, (channels, deep), 1)
    goes = jnp.zeros((channels, deep), jnp.int32)
    for k in range(chan):
        local = channel - flip(z, k) * blk
        goes = jnp.where((local >= 0) & (local < blk), local + k * ring, goes)
    total = jnp.zeros((9 * pad, deep), F32)
    for c in range(3):
        total = total + jnp.dot(
            wt[c], jnp.where(spot == goes + c * some, 1.0, 0.0).astype(BF),
            preferred_element_type=F32)
    wf[...] = total.astype(BF)

    row = lax.broadcasted_iota(jnp.int32, (ring, wide), 0)
    col = lax.broadcasted_iota(jnp.int32, (ring, wide), 1)
    for g in range(groups):
        for k in range(begin[g], begin[g + 1]):
            at = (k - begin[g]) * ring
            for c in range(3):
                own = row - c * some
                hit = (own >= 0) & (own < blk) & (col == own + flip(z, k) * blk)
                place_q[g][at:at + ring, c * wide:(c + 1) * wide] = (
                    jnp.where(hit, 1.0, 0.0).astype(BF))

    last = groups - 1
    pairs = [send(csend[g], crecv[g], c_s.at[g], c_r.at[g], {"space": flip(e, 1)})
             for g in range(last)]

    def reach(g):
        return range(1 if g == last else 2, space, 1 if g == last else 2)

    def piece_of(g, m):
        return csend[g] if m % 2 else wall[g].at[e]

    shares = [[send(piece_of(g, m), wall[g].at[e], w_s.at[g, m], w_r.at[g, m],
                    {"space": flip(e, m)}) for m in reversed(reach(g))]
              for g in range(groups)]
    passes = [send(full[g].at[core], full[g].at[core], f_s.at[g], f_r.at[g],
                   {"space": flip(e, 1)}) for g in range(groups)]

    def my_half(g, which):
        half = full[g].shape[2]
        return wflat[g][:, pl.ds(pl.multiple_of(which * half, LANE), half)]

    def share(g):
        for b in range(3):
            one = lax.dot_general(
                xg[3 * pad:6 * pad, :],
                x3[begin[g] * ring:begin[g + 1] * ring, b * LANE:b * LANE + span],
                ROWS_T, preferred_element_type=F32)
            for a in range(3):
                wflat[g][a * some:(a + 1) * some, b * each[g]:(b + 1) * each[g]] = (
                    one[a * pad:a * pad + some, :])
        csend[g][...] = my_half(g, 1 - core).astype(BF)
        if g == last:
            wall[g][e] = my_half(g, core).astype(BF)
            for c in shares[g]:
                c.start()
        else:
            pairs[g].start()

    def spread(g):
        if g == last:
            return
        pairs[g].wait_recv()
        wall[g][e] = (my_half(g, core) + crecv[g][...].astype(F32)).astype(BF)
        for c in shares[g]:
            c.start()

    def gather_up(g):
        for c in shares[g]:
            c.wait_recv()
        if g == last:
            total = wall[g][0].astype(F32)
            for origin in range(1, space):
                total = total + wall[g][origin].astype(F32)
        else:
            total = wall[g][core].astype(F32)
            for chip in range(1, space // 2):
                total = total + wall[g][2 * chip + core].astype(F32)
        full[g][core] = total.astype(BF)
        passes[g].start()

    def collect(g):
        passes[g].wait_recv()
        both = jnp.concatenate([full[g][0], full[g][1]], axis=1)
        for b in range(3):
            stack[g][b * tall:(b + 1) * tall, 0:each[g]] = both[:, b * each[g]:(b + 1) * each[g]]
        moved = jnp.dot(stack[g][...], place_q[g][...], preferred_element_type=F32)
        acc[...] = moved if g == 0 else acc[...] + moved

    pl.when(has_down)(halo_up.wait_recv)
    fill_signal(2, halo[0])
    pl.when(has_up)(halo_down.wait_recv)
    fill_signal(0, halo[1])

    def shifted(count, first_row, group, h):
        def piece(b, hh):
            at = first_row + b * group
            return r32[at:at + count, hh * LANE:(hh + 1) * LANE]
        v = piece(1, h)
        if h > 0:
            v = v + piece(0, h - 1)
        if h < height - 1:
            v = v + piece(2, h + 1)
        return v

    r32[0:3 * channels, :] = jnp.dot(wb[...], xg[...], preferred_element_type=F32)
    for h in range(height):
        part[pl.ds(h, channels, stride=height), :] = shifted(channels, 0, channels, h)

    def block_of(t):
        return part[pl.ds(pl.multiple_of(t * rows, 16), rows), :]

    def on(where):
        return lambda step: pl.when(where)(step)

    always = lambda step: step()
    if chan == 4:
        inner = lax.rem(lax.div(z + 1, 2), 2) == 1
        gives, takes = on(jnp.logical_not(inner)), on(inner)
        given = [flip(z, 3), flip(z, 2)]
        owners = [flip(z, 2), flip(z, 3)]
        slots = [0, 0]
    else:
        gives = takes = always
        given = [flip(z, 2 * k + 1) for k in range(1, chan // 2)]
        owners = [flip(z, 2 * k) for k in range(1, chan // 2)]
        slots = list(range(chan // 2 - 1))
    next_z = {"chan": flip(z, 1)}
    far = [send(nsend.at[k], nrecv.at[k], n_s.at[k], n_r.at[k], next_z)
           for k in range(1, len(given) + 1)]
    near = send(nsend.at[0], nrecv.at[0], n_s.at[0], n_r.at[0], next_z)
    sums = [send(rsend.at[k], rrecv.at[slot], r_s.at[k], r_r.at[slot], {"chan": owner})
            for k, (slot, owner) in enumerate(zip(slots, owners))]

    def give():
        for k, t in enumerate(given):
            nsend[k + 1] = block_of(t).astype(BF)
            far[k].start()

    def take():
        for k, owner in enumerate(owners):
            far[k].wait_recv()
            rsend[k] = (block_of(owner) + nrecv[k + 1].astype(F32)).astype(BF)
            sums[k].start()

    nsend[0] = block_of(flip(z, 1)).astype(BF)
    gives(give)

    def pass_on():
        takes(take)

    for g in range(groups):
        for k in range(max(begin[g], 1), begin[g + 1]):
            gathers[k].wait_recv()
            if k == chan - 2:
                takes(near.start)
            if k == chan - 1 and chan == 4:
                gives(near.start)
            fill_source(k)
        share(g)
        if g < groups - 1:
            spread(g)

    pass_on()
    spread(groups - 1)
    r32[0:9 * pad, :] = jnp.dot(wf[...], x3[:, LANE:LANE + span], preferred_element_type=F32)

    def relay(a):
        for h in range(height):
            t32[a, pl.ds(h, pad, stride=height), :] = shifted(pad, a * pad, 3 * pad, h)

    relay(0)
    psend[0] = t32[0, 0:rows, :].astype(BF)
    pair = (send(psend.at[0], precv.at[0], p_s.at[0], p_r.at[0], {"space": up}),
            send(psend.at[1], precv.at[1], p_s.at[1], p_r.at[1], {"space": down}))
    pl.when(has_up)(pair[0].start)
    relay(2)
    psend[1] = t32[2, 0:rows, :].astype(BF)
    pl.when(has_down)(pair[1].start)
    for k in range(groups - 1):
        gather_up(k)
    relay(1)

    for k in range(groups - 1):
        collect(k)
    gather_up(groups - 1)
    pl.when(has_down)(pair[0].wait_recv)
    pl.when(has_up)(pair[1].wait_recv)
    out_ref[...] = (t32[1, 0:rows, :] + precv[0].astype(F32)
                    + precv[1].astype(F32)).astype(BF)

    collect(groups - 1)
    for a in range(3):
        for b in range(3):
            for c in range(3):
                at = b * tall + a * some
                wg_ref[(a * 3 + b) * 3 + c] = (
                    acc[at:at + blk, c * wide:c * wide + channels] * scale)

    near.wait_recv()
    total = block_of(z) + nrecv[0].astype(F32)
    for slot in sorted(set(slots)):
        sums[slot].wait_recv()
        total = total + rrecv[slot].astype(F32)
    back_ref[...] = total.astype(BF)

    for c in gathers[1:] + [near] + pairs + passes:
        c.wait_send()

    def given_sent():
        for c in far:
            c.wait_send()

    def sums_sent():
        for c in sums:
            c.wait_send()

    gives(given_sent)
    takes(sums_sent)
    for group in shares:
        for c in group:
            c.wait_send()
    for c in (halo_up, pair[0]):
        pl.when(has_up)(c.wait_send)
    for c in (halo_down, pair[1]):
        pl.when(has_down)(c.wait_send)


def write(*refs):
    n = len(refs) // 2
    copies = [pltpu.make_async_copy(refs[i], refs[n + i], refs[-1].at[i]) for i in range(n)]
    for c in copies:
        c.start()
    for c in copies:
        c.wait()


def body(space, chan, activation, weights, cotangent):
    planes, blk, height, width = activation.shape
    channels = weights.shape[3]
    assert planes == 1 and width == LANE
    pad = up_to(blk, 16)
    rows = blk * height
    cuts = [chan // 2, chan // 4, chan // 4]
    scale = 1.0 / math.sqrt(planes * space * height * width)
    dma = pltpu.SemaphoreType.DMA
    vm = pltpu.VMEM
    some = up_to(blk, 8)
    ring = up_to(3 * some, 16)
    deep = ring * chan
    tall = ring
    flats = [up_to(n * ring, LANE) for n in cuts]
    halves = [up_to(3 * n * ring, 2 * LANE) // 2 for n in cuts]
    groups = len(cuts)
    wide = up_to(channels, LANE)
    shapes = (
        jax.ShapeDtypeStruct((rows, LANE), BF),
        jax.ShapeDtypeStruct((rows, LANE), BF),
        jax.ShapeDtypeStruct((27, blk, channels), F32),
    )
    outs = pl.pallas_call(
        functools.partial(kernel, space, chan, blk, pad, channels, height, cuts, scale),
        out_shape=shapes,
        in_specs=[pl.BlockSpec(memory_space=pltpu.HBM)] * 3,
        out_specs=[pl.BlockSpec(memory_space=vm)] * 3,
        scratch_shapes=[
            vm((chan, rows, LANE), BF),
            vm((rows, LANE), BF),
            vm((27, channels, channels), BF),
            vm((deep, (height + 2) * LANE), BF),
            vm((9 * pad, height * LANE), BF),
            vm((3, 9 * pad, channels), BF),
            vm((9 * pad, deep), BF),
            vm((3 * channels, 9 * pad), BF),
            vm((3, pad * height, LANE), F32),
            vm((3, pad * height, LANE), F32),
            vm((max(9 * pad, 3 * channels), height * LANE), F32),
            vm((channels * height, LANE), F32),
            vm((2, rows, LANE), BF),
            vm((2, rows, LANE), BF),
            vm((2, rows, LANE), BF),
            tuple(vm((tall, 2 * half), F32) for half in halves),
            tuple(vm((tall, half), BF) for half in halves),
            tuple(vm((tall, half), BF) for half in halves),
            tuple(vm((space, tall, half), BF) for half in halves),
            tuple(vm((2, tall, half), BF) for half in halves),
            tuple(vm((3 * tall, flat), BF) for flat in flats),
            vm((3 * tall, 3 * wide), F32),
            tuple(vm((flat, 3 * wide), BF) for flat in flats),
            vm((chan // 2 + 1, rows, LANE), BF),
            vm((chan // 2 + 1, rows, LANE), BF),
            vm((chan // 2, rows, LANE), BF),
            vm((chan // 2, rows, LANE), BF),
            dma((3,)), dma((chan,)), dma((chan,)), dma((2,)), dma((2,)), dma((2,)), dma((2,)),
            dma((groups,)), dma((groups,)), dma((groups, space)), dma((groups, space)),
            dma((groups,)), dma((groups,)),
            dma((chan // 2 + 1,)), dma((chan // 2 + 1,)), dma((chan // 2,)), dma((chan // 2,)),
        ],
        compiler_params=pltpu.CompilerParams(
            collective_id=0, has_side_effects=True, vmem_limit_bytes=40 * 2**20),
    )(*[pltpu.with_memory_space_constraint(x, pltpu.HBM) for x in (
        activation.reshape(rows, width), cotangent.reshape(rows, width),
        weights.reshape(27, channels, channels))])
    out, back, grads = pl.pallas_call(
        write,
        out_shape=shapes,
        in_specs=[pl.BlockSpec(memory_space=vm)] * 3,
        out_specs=[pl.BlockSpec(memory_space=pltpu.HBM)] * 3,
        scratch_shapes=[dma((3,))],
        compiler_params=pltpu.CompilerParams(vmem_limit_bytes=2**20),
    )(*outs)
    field = (1, blk, height, width)
    grads = jnp.swapaxes(grads.reshape(3, 3, 3, blk, channels), 3, 4)
    return out.reshape(field), back.reshape(field), grads


def solution(mesh):
    field = P("space", "chan", None, None)
    return jax.shard_map(
        functools.partial(body, mesh.shape["space"], mesh.shape["chan"]),
        mesh=mesh,
        in_specs=(field, P(), field),
        out_specs=(field, field, P(None, None, None, None, "chan")),
        check_vma=False,
    )
```

```python
import functools
import math

import jax
import jax.numpy as jnp
from jax import lax
from jax.experimental import pallas as pl
from jax.experimental.pallas import tpu as pltpu
from jax.sharding import PartitionSpec as P

BF, F32 = jnp.bfloat16, jnp.float32
LANE = 128
ROWS_T = (((1,), (1,)), ((), ()))


def up_to(n, m):
    return -(-n // m) * m


def flip(i, m):
    out = i
    for b in range(m.bit_length()):
        if m >> b & 1:
            bit = lax.rem(lax.div(i, 1 << b), 2)
            out = out + (1 << b) * (1 - 2 * bit)
    return out


def kernel(space, chan, blk, pad, channels, height, cuts, scale,
           a_hbm, g_hbm, w_hbm, out_ref, back_ref, wg_ref,
           ga, gv, w_ref, x3, xs, xg, wt, wf, wb, z32, t32, r32, part,
           halo, psend, precv, wflat, csend, crecv, wall, full, stack, acc, place_q,
           nsend, nrecv, rsend, rrecv,
           l_s, g_s, g_r, h_s, h_r, p_s, p_r, c_s, c_r, w_s, w_r, f_s, f_r, n_s, n_r, r_s, r_r):
    e = lax.axis_index("space")
    z = lax.axis_index("chan")
    rows = blk * height
    span = height * LANE
    groups = len(cuts)
    begin = [sum(cuts[:g]) for g in range(groups + 1)]
    tall = full[0].shape[1]
    some = up_to(blk, 8)
    ring = up_to(3 * some, 16)
    each = [n * ring for n in cuts]
    wide = acc.shape[1] // 3
    up, down = lax.rem(e + 1, space), lax.rem(e + space - 1, space)
    core = lax.rem(e, 2)

    barrier = pltpu.get_barrier_semaphore()
    others = [{"chan": flip(z, k)} for k in range(1, chan)]
    others += [{"space": flip(e, k)} for k in range(1, space)]
    for other in others:
        pl.semaphore_signal(barrier, inc=1, device_id=other)
    loads = [pltpu.make_async_copy(a_hbm, ga.at[0], l_s.at[1]),
             pltpu.make_async_copy(g_hbm, gv, l_s.at[0]),
             pltpu.make_async_copy(w_hbm, w_ref, l_s.at[2])]
    for c in loads:
        c.start()

    def send(src, dst, ssem, rsem, to):
        return pltpu.make_async_remote_copy(src, dst, ssem, rsem, device_id=to)

    gathers = [None] + [
        send(ga.at[0], ga.at[k], g_s.at[k], g_r.at[k], {"chan": flip(z, k)})
        for k in range(1, chan)]
    halo_up = send(gv, halo.at[0], h_s.at[0], h_r.at[0], {"space": up})
    halo_down = send(gv, halo.at[1], h_s.at[1], h_r.at[1], {"space": down})
    has_up, has_down = e < space - 1, e > 0

    pl.semaphore_wait(barrier, len(others))
    loads[0].wait()
    for c in gathers[1:]:
        c.start()
    loads[1].wait()
    pl.when(has_up)(halo_up.start)
    pl.when(has_down)(halo_down.start)

    def no_lower():
        halo[0] = jnp.zeros((rows, LANE), BF)
        precv[0] = jnp.zeros((rows, LANE), BF)

    def no_upper():
        halo[1] = jnp.zeros((rows, LANE), BF)
        precv[1] = jnp.zeros((rows, LANE), BF)

    pl.when(e == 0)(no_lower)
    pl.when(e == space - 1)(no_upper)

    z32[...] = jnp.zeros_like(z32)
    for g in range(groups):
        xs[g][0:each[g], 0:LANE] = jnp.zeros((each[g], LANE), BF)
        xs[g][2 * each[g]:3 * each[g], span - LANE:span] = jnp.zeros((each[g], LANE), BF)
    for ref in (*wflat, *stack, *place_q):
        ref[...] = jnp.zeros_like(ref)
    few = lax.broadcasted_iota(jnp.int32, (rows, LANE), 1)

    def shift(src):
        v = src.astype(F32)
        z32[0, 0:rows, :] = jnp.where(few == 0, 0.0, pltpu.roll(v, 1, 1))
        z32[1, 0:rows, :] = v
        z32[2, 0:rows, :] = jnp.where(few == LANE - 1, 0.0, pltpu.roll(v, LANE - 1, 1))

    def fill_signal(a, src):
        shift(src)
        for c in range(3):
            at = (c * 3 + a) * pad
            for h in range(height):
                xg[at:at + pad, h * LANE:(h + 1) * LANE] = (
                    z32[c, pl.ds(h, pad, stride=height), :].astype(BF))

    def fill_source(k):
        shift(ga[k])
        g = max(g for g in range(groups) if begin[g] <= k)
        rest = [jnp.zeros((ring - 3 * some, LANE), F32)] if ring > 3 * some else []
        for h in range(height):
            taps = [z32[c, pl.ds(h, some, stride=height), :] for c in range(3)]
            piece = jnp.concatenate(taps + rest, axis=0).astype(BF)
            x3[k * ring:(k + 1) * ring, h * LANE:(h + 1) * LANE] = piece
            for b in range(3):
                to = h + 1 - b
                if 0 <= to < height:
                    at = b * each[g] + (k - begin[g]) * ring
                    xs[g][at:at + ring, to * LANE:(to + 1) * LANE] = piece

    fill_signal(1, gv[...])
    fill_source(0)

    loads[2].wait()
    thick = 9 * pad
    first = lax.broadcasted_iota(jnp.int32, (channels, thick), 0) - z * blk
    place = lax.broadcasted_iota(jnp.int32, (channels, thick), 1)
    inside = (first >= 0) & (first < blk)
    for b in range(3):
        total = jnp.zeros((channels, thick), F32)
        for c in range(3):
            for a in range(3):
                spot = inside & (place == first + (c * 3 + a) * pad)
                tap = w_ref[(a * 3 + 2 - b) * 3 + 2 - c]
                total = total + jnp.dot(
                    tap, jnp.where(spot, 1.0, 0.0).astype(BF), preferred_element_type=F32)
        wb[b * channels:(b + 1) * channels, :] = total.astype(BF)

    row = lax.broadcasted_iota(jnp.int32, (pad, channels), 0)
    col = lax.broadcasted_iota(jnp.int32, (pad, channels), 1)
    pick = jnp.where((col == row + z * blk) & (row < blk), 1.0, 0.0).astype(BF)
    for a in range(3):
        for b in range(3):
            for c in range(3):
                at = (b * 3 + a) * pad
                wt[c, at:at + pad, :] = lax.dot_general(
                    pick, w_ref[(a * 3 + b) * 3 + c], ROWS_T,
                    preferred_element_type=F32).astype(BF)
    deep = x3.shape[0]
    channel = lax.broadcasted_iota(jnp.int32, (channels, deep), 0)
    spot = lax.broadcasted_iota(jnp.int32, (channels, deep), 1)
    goes = jnp.zeros((channels, deep), jnp.int32)
    for k in range(chan):
        local = channel - flip(z, k) * blk
        goes = jnp.where((local >= 0) & (local < blk), local + k * ring, goes)
    total = jnp.zeros((9 * pad, deep), F32)
    for c in range(3):
        total = total + jnp.dot(
            wt[c], jnp.where(spot == goes + c * some, 1.0, 0.0).astype(BF),
            preferred_element_type=F32)
    wf[...] = total.astype(BF)

    row = lax.broadcasted_iota(jnp.int32, (ring, wide), 0)
    col = lax.broadcasted_iota(jnp.int32, (ring, wide), 1)
    for g in range(groups):
        for k in range(begin[g], begin[g + 1]):
            at = (k - begin[g]) * ring
            for c in range(3):
                own = row - c * some
                hit = (own >= 0) & (own < blk) & (col == own + flip(z, k) * blk)
                place_q[g][at:at + ring, c * wide:(c + 1) * wide] = (
                    jnp.where(hit, 1.0, 0.0).astype(BF))

    last = groups - 1
    pairs = [send(csend[g], crecv[g], c_s.at[g], c_r.at[g], {"space": flip(e, 1)})
             for g in range(last)]

    def reach(g):
        return range(1 if g == last else 2, space, 1 if g == last else 2)

    def piece_of(g, m):
        return csend[g] if m % 2 else wall[g].at[e]

    shares = [[send(piece_of(g, m), wall[g].at[e], w_s.at[g, m], w_r.at[g, m],
                    {"space": flip(e, m)}) for m in reversed(reach(g))]
              for g in range(groups)]
    passes = [send(full[g].at[core], full[g].at[core], f_s.at[g], f_r.at[g],
                   {"space": flip(e, 1)}) for g in range(groups)]

    def my_half(g, which):
        half = full[g].shape[2]
        return wflat[g][:, pl.ds(pl.multiple_of(which * half, LANE), half)]

    def share(g):
        one = lax.dot_general(
            xg[3 * pad:6 * pad, :], xs[g][...], ROWS_T, preferred_element_type=F32)
        for a in range(3):
            wflat[g][a * some:(a + 1) * some, 0:3 * each[g]] = one[a * pad:a * pad + some, :]
        csend[g][...] = my_half(g, 1 - core).astype(BF)
        if g == last:
            wall[g][e] = my_half(g, core).astype(BF)
            for c in shares[g]:
                c.start()
        else:
            pairs[g].start()

    def spread(g):
        if g == last:
            return
        pairs[g].wait_recv()
        wall[g][e] = (my_half(g, core) + crecv[g][...].astype(F32)).astype(BF)
        for c in shares[g]:
            c.start()

    def gather_up(g):
        for c in shares[g]:
            c.wait_recv()
        if g == last:
            total = wall[g][0].astype(F32)
            for origin in range(1, space):
                total = total + wall[g][origin].astype(F32)
        else:
            total = wall[g][core].astype(F32)
            for chip in range(1, space // 2):
                total = total + wall[g][2 * chip + core].astype(F32)
        full[g][core] = total.astype(BF)
        passes[g].start()

    def collect(g):
        passes[g].wait_recv()
        both = jnp.concatenate([full[g][0], full[g][1]], axis=1)
        for b in range(3):
            stack[g][b * tall:(b + 1) * tall, 0:each[g]] = both[:, b * each[g]:(b + 1) * each[g]]
        moved = jnp.dot(stack[g][...], place_q[g][...], preferred_element_type=F32)
        acc[...] = moved if g == 0 else acc[...] + moved

    pl.when(has_down)(halo_up.wait_recv)
    fill_signal(2, halo[0])
    pl.when(has_up)(halo_down.wait_recv)
    fill_signal(0, halo[1])

    def shifted(count, first_row, group, h):
        def piece(b, hh):
            at = first_row + b * group
            return r32[at:at + count, hh * LANE:(hh + 1) * LANE]
        v = piece(1, h)
        if h > 0:
            v = v + piece(0, h - 1)
        if h < height - 1:
            v = v + piece(2, h + 1)
        return v

    r32[0:3 * channels, :] = jnp.dot(wb[...], xg[...], preferred_element_type=F32)
    for h in range(height):
        part[pl.ds(h, channels, stride=height), :] = shifted(channels, 0, channels, h)

    def block_of(t):
        return part[pl.ds(pl.multiple_of(t * rows, 16), rows), :]

    def on(where):
        return lambda step: pl.when(where)(step)

    always = lambda step: step()
    if chan == 4:
        inner = lax.rem(lax.div(z + 1, 2), 2) == 1
        gives, takes = on(jnp.logical_not(inner)), on(inner)
        given = [flip(z, 3), flip(z, 2)]
        owners = [flip(z, 2), flip(z, 3)]
        slots = [0, 0]
    else:
        gives = takes = always
        given = [flip(z, 2 * k + 1) for k in range(1, chan // 2)]
        owners = [flip(z, 2 * k) for k in range(1, chan // 2)]
        slots = list(range(chan // 2 - 1))
    next_z = {"chan": flip(z, 1)}
    far = [send(nsend.at[k], nrecv.at[k], n_s.at[k], n_r.at[k], next_z)
           for k in range(1, len(given) + 1)]
    near = send(nsend.at[0], nrecv.at[0], n_s.at[0], n_r.at[0], next_z)
    sums = [send(rsend.at[k], rrecv.at[slot], r_s.at[k], r_r.at[slot], {"chan": owner})
            for k, (slot, owner) in enumerate(zip(slots, owners))]

    def give():
        for k, t in enumerate(given):
            nsend[k + 1] = block_of(t).astype(BF)
            far[k].start()

    def take():
        for k, owner in enumerate(owners):
            far[k].wait_recv()
            rsend[k] = (block_of(owner) + nrecv[k + 1].astype(F32)).astype(BF)
            sums[k].start()

    nsend[0] = block_of(flip(z, 1)).astype(BF)
    gives(give)

    def pass_on():
        takes(take)

    for g in range(groups):
        for k in range(max(begin[g], 1), begin[g + 1]):
            gathers[k].wait_recv()
            if k == chan - 2:
                takes(near.start)
            if k == chan - 1 and chan == 4:
                gives(near.start)
            fill_source(k)
        share(g)
        if g < groups - 1:
            spread(g)

    pass_on()
    spread(groups - 1)
    r32[0:9 * pad, :] = jnp.dot(wf[...], x3[...], preferred_element_type=F32)

    def relay(a):
        for h in range(height):
            t32[a, pl.ds(h, pad, stride=height), :] = shifted(pad, a * pad, 3 * pad, h)

    relay(0)
    psend[0] = t32[0, 0:rows, :].astype(BF)
    pair = (send(psend.at[0], precv.at[0], p_s.at[0], p_r.at[0], {"space": up}),
            send(psend.at[1], precv.at[1], p_s.at[1], p_r.at[1], {"space": down}))
    pl.when(has_up)(pair[0].start)
    relay(2)
    psend[1] = t32[2, 0:rows, :].astype(BF)
    pl.when(has_down)(pair[1].start)
    for k in range(groups - 1):
        gather_up(k)
    relay(1)

    for k in range(groups - 1):
        collect(k)
    gather_up(groups - 1)
    pl.when(has_down)(pair[0].wait_recv)
    pl.when(has_up)(pair[1].wait_recv)
    out_ref[...] = (t32[1, 0:rows, :] + precv[0].astype(F32)
                    + precv[1].astype(F32)).astype(BF)

    collect(groups - 1)
    for a in range(3):
        for b in range(3):
            for c in range(3):
                at = b * tall + a * some
                wg_ref[(a * 3 + b) * 3 + c] = (
                    acc[at:at + blk, c * wide:c * wide + channels] * scale)

    near.wait_recv()
    total = block_of(z) + nrecv[0].astype(F32)
    for slot in sorted(set(slots)):
        sums[slot].wait_recv()
        total = total + rrecv[slot].astype(F32)
    back_ref[...] = total.astype(BF)

    for c in gathers[1:] + [near] + pairs + passes:
        c.wait_send()

    def given_sent():
        for c in far:
            c.wait_send()

    def sums_sent():
        for c in sums:
            c.wait_send()

    gives(given_sent)
    takes(sums_sent)
    for group in shares:
        for c in group:
            c.wait_send()
    for c in (halo_up, pair[0]):
        pl.when(has_up)(c.wait_send)
    for c in (halo_down, pair[1]):
        pl.when(has_down)(c.wait_send)


def write(*refs):
    n = len(refs) // 2
    copies = [pltpu.make_async_copy(refs[i], refs[n + i], refs[-1].at[i]) for i in range(n)]
    for c in reversed(copies):
        c.start()
    for c in copies:
        c.wait()


def body(space, chan, activation, weights, cotangent):
    planes, blk, height, width = activation.shape
    channels = weights.shape[3]
    assert planes == 1 and width == LANE
    pad = up_to(blk, 16)
    rows = blk * height
    cuts = [chan // 2, chan // 4, chan // 4]
    scale = 1.0 / math.sqrt(planes * space * height * width)
    dma = pltpu.SemaphoreType.DMA
    vm = pltpu.VMEM
    some = up_to(blk, 8)
    ring = up_to(3 * some, 16)
    deep = ring * chan
    tall = ring
    flats = [up_to(n * ring, LANE) for n in cuts]
    halves = [up_to(3 * n * ring, 2 * LANE) // 2 for n in cuts]
    groups = len(cuts)
    wide = up_to(channels, LANE)
    shapes = (
        jax.ShapeDtypeStruct((rows, LANE), BF),
        jax.ShapeDtypeStruct((rows, LANE), BF),
        jax.ShapeDtypeStruct((27, blk, channels), F32),
    )
    outs = pl.pallas_call(
        functools.partial(kernel, space, chan, blk, pad, channels, height, cuts, scale),
        out_shape=shapes,
        in_specs=[pl.BlockSpec(memory_space=pltpu.HBM)] * 3,
        out_specs=[pl.BlockSpec(memory_space=vm)] * 3,
        scratch_shapes=[
            vm((chan, rows, LANE), BF),
            vm((rows, LANE), BF),
            vm((27, channels, channels), BF),
            vm((deep, height * LANE), BF),
            tuple(vm((3 * n * ring, height * LANE), BF) for n in cuts),
            vm((9 * pad, height * LANE), BF),
            vm((3, 9 * pad, channels), BF),
            vm((9 * pad, deep), BF),
            vm((3 * channels, 9 * pad), BF),
            vm((3, pad * height, LANE), F32),
            vm((3, pad * height, LANE), F32),
            vm((max(9 * pad, 3 * channels), height * LANE), F32),
            vm((channels * height, LANE), F32),
            vm((2, rows, LANE), BF),
            vm((2, rows, LANE), BF),
            vm((2, rows, LANE), BF),
            tuple(vm((tall, 2 * half), F32) for half in halves),
            tuple(vm((tall, half), BF) for half in halves),
            tuple(vm((tall, half), BF) for half in halves),
            tuple(vm((space, tall, half), BF) for half in halves),
            tuple(vm((2, tall, half), BF) for half in halves),
            tuple(vm((3 * tall, flat), BF) for flat in flats),
            vm((3 * tall, 3 * wide), F32),
            tuple(vm((flat, 3 * wide), BF) for flat in flats),
            vm((chan // 2 + 1, rows, LANE), BF),
            vm((chan // 2 + 1, rows, LANE), BF),
            vm((chan // 2, rows, LANE), BF),
            vm((chan // 2, rows, LANE), BF),
            dma((3,)), dma((chan,)), dma((chan,)), dma((2,)), dma((2,)), dma((2,)), dma((2,)),
            dma((groups,)), dma((groups,)), dma((groups, space)), dma((groups, space)),
            dma((groups,)), dma((groups,)),
            dma((chan // 2 + 1,)), dma((chan // 2 + 1,)), dma((chan // 2,)), dma((chan // 2,)),
        ],
        compiler_params=pltpu.CompilerParams(
            collective_id=0, has_side_effects=True, vmem_limit_bytes=40 * 2**20),
    )(*[pltpu.with_memory_space_constraint(x, pltpu.HBM) for x in (
        activation.reshape(rows, width), cotangent.reshape(rows, width),
        weights.reshape(27, channels, channels))])
    out, back, grads = pl.pallas_call(
        write,
        out_shape=shapes,
        in_specs=[pl.BlockSpec(memory_space=vm)] * 3,
        out_specs=[pl.BlockSpec(memory_space=pltpu.HBM)] * 3,
        scratch_shapes=[dma((3,))],
        compiler_params=pltpu.CompilerParams(vmem_limit_bytes=2**20),
    )(*outs)
    field = (1, blk, height, width)
    grads = jnp.swapaxes(grads.reshape(3, 3, 3, blk, channels), 3, 4)
    return out.reshape(field), back.reshape(field), grads


def solution(mesh):
    field = P("space", "chan", None, None)
    return jax.shard_map(
        functools.partial(body, mesh.shape["space"], mesh.shape["chan"]),
        mesh=mesh,
        in_specs=(field, P(), field),
        out_specs=(field, field, P(None, None, None, None, "chan")),
        check_vma=False,
    )
```

```python
import functools
import math

import jax
import jax.numpy as jnp
from jax import lax
from jax.experimental import pallas as pl
from jax.experimental.pallas import tpu as pltpu
from jax.sharding import PartitionSpec as P

BF, F32 = jnp.bfloat16, jnp.float32
LANE = 128
ROWS_T = (((1,), (1,)), ((), ()))


def up_to(n, m):
    return -(-n // m) * m


def flip(i, m):
    out = i
    for b in range(m.bit_length()):
        if m >> b & 1:
            bit = lax.rem(lax.div(i, 1 << b), 2)
            out = out + (1 << b) * (1 - 2 * bit)
    return out


def kernel(space, chan, blk, pad, channels, height, cuts, scale,
           a_hbm, g_hbm, w_hbm, out_ref, back_ref, wg_ref,
           ga, gv, w_ref, x3, xg, wt, wf, wb, z32, t32, r32, part,
           halo, psend, precv, wflat, csend, crecv, wall, full, stack, acc, place_q,
           nsend, nrecv, rsend, rrecv,
           l_s, g_s, g_r, h_s, h_r, p_s, p_r, c_s, c_r, w_s, w_r, f_s, f_r, n_s, n_r, r_s, r_r):
    e = lax.axis_index("space")
    z = lax.axis_index("chan")
    rows = blk * height
    span = height * LANE
    groups = len(cuts)
    begin = [sum(cuts[:g]) for g in range(groups + 1)]
    tall = full[0].shape[1]
    some = up_to(blk, 8)
    ring = up_to(3 * some, 16)
    each = [n * ring for n in cuts]
    wide = acc.shape[1] // 3
    up, down = lax.rem(e + 1, space), lax.rem(e + space - 1, space)
    core = lax.rem(e, 2)

    barrier = pltpu.get_barrier_semaphore()
    others = [{"chan": flip(z, k)} for k in range(1, chan)]
    others += [{"space": flip(e, k)} for k in range(1, space)]
    for other in others:
        pl.semaphore_signal(barrier, inc=1, device_id=other)
    loads = [pltpu.make_async_copy(a_hbm, ga.at[0], l_s.at[1]),
             pltpu.make_async_copy(g_hbm, gv, l_s.at[0]),
             pltpu.make_async_copy(w_hbm, w_ref, l_s.at[2])]
    for c in loads:
        c.start()

    def send(src, dst, ssem, rsem, to):
        return pltpu.make_async_remote_copy(src, dst, ssem, rsem, device_id=to)

    gathers = [None] + [
        send(ga.at[0], ga.at[k], g_s.at[k], g_r.at[k], {"chan": flip(z, k)})
        for k in range(1, chan)]
    halo_up = send(gv, halo.at[0], h_s.at[0], h_r.at[0], {"space": up})
    halo_down = send(gv, halo.at[1], h_s.at[1], h_r.at[1], {"space": down})
    has_up, has_down = e < space - 1, e > 0

    pl.semaphore_wait(barrier, len(others))
    loads[0].wait()
    for c in gathers[1:]:
        c.start()
    loads[1].wait()
    pl.when(has_up)(halo_up.start)
    pl.when(has_down)(halo_down.start)

    def no_lower():
        halo[0] = jnp.zeros((rows, LANE), BF)
        precv[0] = jnp.zeros((rows, LANE), BF)

    def no_upper():
        halo[1] = jnp.zeros((rows, LANE), BF)
        precv[1] = jnp.zeros((rows, LANE), BF)

    pl.when(e == 0)(no_lower)
    pl.when(e == space - 1)(no_upper)

    z32[...] = jnp.zeros_like(z32)
    x3[:, 0:LANE] = jnp.zeros((x3.shape[0], LANE), BF)
    x3[:, span + LANE:span + 2 * LANE] = jnp.zeros((x3.shape[0], LANE), BF)
    for ref in (*wflat, *stack, *place_q):
        ref[...] = jnp.zeros_like(ref)
    few = lax.broadcasted_iota(jnp.int32, (rows, LANE), 1)

    def shift(src):
        v = src.astype(F32)
        z32[0, 0:rows, :] = jnp.where(few == 0, 0.0, pltpu.roll(v, 1, 1))
        z32[1, 0:rows, :] = v
        z32[2, 0:rows, :] = jnp.where(few == LANE - 1, 0.0, pltpu.roll(v, LANE - 1, 1))

    def fill_signal(a, src):
        shift(src)
        for c in range(3):
            at = (c * 3 + a) * pad
            for h in range(height):
                xg[at:at + pad, h * LANE:(h + 1) * LANE] = (
                    z32[c, pl.ds(h, pad, stride=height), :].astype(BF))

    def fill_source(k):
        shift(ga[k])
        rest = [jnp.zeros((ring - 3 * some, LANE), F32)] if ring > 3 * some else []
        for h in range(height):
            taps = [z32[c, pl.ds(h, some, stride=height), :] for c in range(3)]
            x3[k * ring:(k + 1) * ring, (h + 1) * LANE:(h + 2) * LANE] = (
                jnp.concatenate(taps + rest, axis=0).astype(BF))

    fill_signal(1, gv[...])
    fill_source(0)

    loads[2].wait()
    thick = 9 * pad
    first = lax.broadcasted_iota(jnp.int32, (channels, thick), 0) - z * blk
    place = lax.broadcasted_iota(jnp.int32, (channels, thick), 1)
    inside = (first >= 0) & (first < blk)
    for b in range(3):
        total = jnp.zeros((channels, thick), F32)
        for c in range(3):
            for a in range(3):
                spot = inside & (place == first + (c * 3 + a) * pad)
                tap = w_ref[(a * 3 + 2 - b) * 3 + 2 - c]
                total = total + jnp.dot(
                    tap, jnp.where(spot, 1.0, 0.0).astype(BF), preferred_element_type=F32)
        wb[b * channels:(b + 1) * channels, :] = total.astype(BF)

    row = lax.broadcasted_iota(jnp.int32, (pad, channels), 0)
    col = lax.broadcasted_iota(jnp.int32, (pad, channels), 1)
    pick = jnp.where((col == row + z * blk) & (row < blk), 1.0, 0.0).astype(BF)
    for a in range(3):
        for b in range(3):
            for c in range(3):
                at = (b * 3 + a) * pad
                wt[c, at:at + pad, :] = lax.dot_general(
                    pick, w_ref[(a * 3 + b) * 3 + c], ROWS_T,
                    preferred_element_type=F32).astype(BF)
    deep = x3.shape[0]
    channel = lax.broadcasted_iota(jnp.int32, (channels, deep), 0)
    spot = lax.broadcasted_iota(jnp.int32, (channels, deep), 1)
    goes = jnp.zeros((channels, deep), jnp.int32)
    for k in range(chan):
        local = channel - flip(z, k) * blk
        goes = jnp.where((local >= 0) & (local < blk), local + k * ring, goes)
    total = jnp.zeros((9 * pad, deep), F32)
    for c in range(3):
        total = total + jnp.dot(
            wt[c], jnp.where(spot == goes + c * some, 1.0, 0.0).astype(BF),
            preferred_element_type=F32)
    wf[...] = total.astype(BF)

    row = lax.broadcasted_iota(jnp.int32, (ring, wide), 0)
    col = lax.broadcasted_iota(jnp.int32, (ring, wide), 1)
    for g in range(groups):
        for k in range(begin[g], begin[g + 1]):
            at = (k - begin[g]) * ring
            for c in range(3):
                own = row - c * some
                hit = (own >= 0) & (own < blk) & (col == own + flip(z, k) * blk)
                place_q[g][at:at + ring, c * wide:(c + 1) * wide] = (
                    jnp.where(hit, 1.0, 0.0).astype(BF))

    last = groups - 1
    pairs = [send(csend[g], crecv[g], c_s.at[g], c_r.at[g], {"space": flip(e, 1)})
             for g in range(last)]

    def reach(g):
        return range(1 if g == last else 2, space, 1 if g == last else 2)

    def piece_of(g, m):
        return csend[g] if m % 2 else wall[g].at[e]

    shares = [[send(piece_of(g, m), wall[g].at[e], w_s.at[g, m], w_r.at[g, m],
                    {"space": flip(e, m)}) for m in reversed(reach(g))]
              for g in range(groups)]
    passes = [send(full[g].at[core], full[g].at[core], f_s.at[g], f_r.at[g],
                   {"space": flip(e, 1)}) for g in range(groups)]

    def my_half(g, which):
        half = full[g].shape[2]
        return wflat[g][:, pl.ds(pl.multiple_of(which * half, LANE), half)]

    def share(g):
        for b in range(3):
            one = lax.dot_general(
                xg[3 * pad:6 * pad, :],
                x3[begin[g] * ring:begin[g + 1] * ring, b * LANE:b * LANE + span],
                ROWS_T, preferred_element_type=F32)
            for a in range(3):
                wflat[g][a * some:(a + 1) * some, b * each[g]:(b + 1) * each[g]] = (
                    one[a * pad:a * pad + some, :])
        csend[g][...] = my_half(g, 1 - core).astype(BF)
        if g == last:
            wall[g][e] = my_half(g, core).astype(BF)
            for c in shares[g]:
                c.start()
        else:
            pairs[g].start()

    def spread(g):
        if g == last:
            return
        pairs[g].wait_recv()
        wall[g][e] = (my_half(g, core) + crecv[g][...].astype(F32)).astype(BF)
        for c in shares[g]:
            c.start()

    def gather_up(g):
        for c in shares[g]:
            c.wait_recv()
        if g == last:
            total = wall[g][0].astype(F32)
            for origin in range(1, space):
                total = total + wall[g][origin].astype(F32)
        else:
            total = wall[g][core].astype(F32)
            for chip in range(1, space // 2):
                total = total + wall[g][2 * chip + core].astype(F32)
        full[g][core] = total.astype(BF)
        passes[g].start()

    def collect(g):
        passes[g].wait_recv()
        both = jnp.concatenate([full[g][0], full[g][1]], axis=1)
        for b in range(3):
            stack[g][b * tall:(b + 1) * tall, 0:each[g]] = both[:, b * each[g]:(b + 1) * each[g]]
        moved = jnp.dot(stack[g][...], place_q[g][...], preferred_element_type=F32)
        acc[...] = moved if g == 0 else acc[...] + moved

    pl.when(has_down)(halo_up.wait_recv)
    fill_signal(2, halo[0])
    pl.when(has_up)(halo_down.wait_recv)
    fill_signal(0, halo[1])

    def shifted(count, first_row, group, h):
        def piece(b, hh):
            at = first_row + b * group
            return r32[at:at + count, hh * LANE:(hh + 1) * LANE]
        v = piece(1, h)
        if h > 0:
            v = v + piece(0, h - 1)
        if h < height - 1:
            v = v + piece(2, h + 1)
        return v

    r32[0:3 * channels, :] = jnp.dot(wb[...], xg[...], preferred_element_type=F32)
    for h in range(height):
        part[pl.ds(h, channels, stride=height), :] = shifted(channels, 0, channels, h)

    def block_of(t):
        return part[pl.ds(pl.multiple_of(t * rows, 16), rows), :]

    def on(where):
        return lambda step: pl.when(where)(step)

    always = lambda step: step()
    if chan == 4:
        inner = lax.rem(lax.div(z + 1, 2), 2) == 1
        gives, takes = on(jnp.logical_not(inner)), on(inner)
        given = [flip(z, 3), flip(z, 2)]
        owners = [flip(z, 2), flip(z, 3)]
        slots = [0, 0]
    else:
        gives = takes = always
        given = [flip(z, 2 * k + 1) for k in range(1, chan // 2)]
        owners = [flip(z, 2 * k) for k in range(1, chan // 2)]
        slots = list(range(chan // 2 - 1))
    next_z = {"chan": flip(z, 1)}
    far = [send(nsend.at[k], nrecv.at[k], n_s.at[k], n_r.at[k], next_z)
           for k in range(1, len(given) + 1)]
    near = send(nsend.at[0], nrecv.at[0], n_s.at[0], n_r.at[0], next_z)
    sums = [send(rsend.at[k], rrecv.at[slot], r_s.at[k], r_r.at[slot], {"chan": owner})
            for k, (slot, owner) in enumerate(zip(slots, owners))]

    def give():
        for k, t in enumerate(given):
            nsend[k + 1] = block_of(t).astype(BF)
            far[k].start()

    def take():
        for k, owner in enumerate(owners):
            far[k].wait_recv()
            rsend[k] = (block_of(owner) + nrecv[k + 1].astype(F32)).astype(BF)
            sums[k].start()

    nsend[0] = block_of(flip(z, 1)).astype(BF)
    def pass_on():
        takes(take)

    for g in range(groups):
        for k in range(max(begin[g], 1), begin[g + 1]):
            gathers[k].wait_recv()
            if k == 1:
                gives(give)
            if k == chan - 2:
                takes(near.start)
            if k == chan - 1 and chan == 4:
                gives(near.start)
            fill_source(k)
        share(g)
        if g < groups - 1:
            spread(g)

    pass_on()
    spread(groups - 1)
    r32[0:9 * pad, :] = jnp.dot(wf[...], x3[:, LANE:LANE + span], preferred_element_type=F32)

    def relay(a):
        for h in range(height):
            t32[a, pl.ds(h, pad, stride=height), :] = shifted(pad, a * pad, 3 * pad, h)

    relay(0)
    psend[0] = t32[0, 0:rows, :].astype(BF)
    pair = (send(psend.at[0], precv.at[0], p_s.at[0], p_r.at[0], {"space": up}),
            send(psend.at[1], precv.at[1], p_s.at[1], p_r.at[1], {"space": down}))
    pl.when(has_up)(pair[0].start)
    relay(2)
    psend[1] = t32[2, 0:rows, :].astype(BF)
    pl.when(has_down)(pair[1].start)
    for k in range(groups - 1):
        gather_up(k)
    relay(1)

    for k in range(groups - 1):
        collect(k)
    gather_up(groups - 1)
    pl.when(has_down)(pair[0].wait_recv)
    pl.when(has_up)(pair[1].wait_recv)
    out_ref[...] = (t32[1, 0:rows, :] + precv[0].astype(F32)
                    + precv[1].astype(F32)).astype(BF)

    collect(groups - 1)
    for a in range(3):
        for b in range(3):
            for c in range(3):
                at = b * tall + a * some
                wg_ref[(a * 3 + b) * 3 + c] = (
                    acc[at:at + blk, c * wide:c * wide + channels] * scale)

    near.wait_recv()
    total = block_of(z) + nrecv[0].astype(F32)
    for slot in sorted(set(slots)):
        sums[slot].wait_recv()
        total = total + rrecv[slot].astype(F32)
    back_ref[...] = total.astype(BF)

    for c in gathers[1:] + [near] + pairs + passes:
        c.wait_send()

    def given_sent():
        for c in far:
            c.wait_send()

    def sums_sent():
        for c in sums:
            c.wait_send()

    gives(given_sent)
    takes(sums_sent)
    for group in shares:
        for c in group:
            c.wait_send()
    for c in (halo_up, pair[0]):
        pl.when(has_up)(c.wait_send)
    for c in (halo_down, pair[1]):
        pl.when(has_down)(c.wait_send)


def write(*refs):
    n = len(refs) // 2
    copies = [pltpu.make_async_copy(refs[i], refs[n + i], refs[-1].at[i]) for i in range(n)]
    for c in copies:
        c.start()
    for c in copies:
        c.wait()


def body(space, chan, activation, weights, cotangent):
    planes, blk, height, width = activation.shape
    channels = weights.shape[3]
    assert planes == 1 and width == LANE
    pad = up_to(blk, 16)
    rows = blk * height
    cuts = [chan // 2, chan // 4, chan // 4]
    scale = 1.0 / math.sqrt(planes * space * height * width)
    dma = pltpu.SemaphoreType.DMA
    vm = pltpu.VMEM
    some = up_to(blk, 8)
    ring = up_to(3 * some, 16)
    deep = ring * chan
    tall = ring
    flats = [up_to(n * ring, LANE) for n in cuts]
    halves = [up_to(3 * n * ring, 2 * LANE) // 2 for n in cuts]
    groups = len(cuts)
    wide = up_to(channels, LANE)
    shapes = (
        jax.ShapeDtypeStruct((rows, LANE), BF),
        jax.ShapeDtypeStruct((rows, LANE), BF),
        jax.ShapeDtypeStruct((27, blk, channels), F32),
    )
    outs = pl.pallas_call(
        functools.partial(kernel, space, chan, blk, pad, channels, height, cuts, scale),
        out_shape=shapes,
        in_specs=[pl.BlockSpec(memory_space=pltpu.HBM)] * 3,
        out_specs=[pl.BlockSpec(memory_space=vm)] * 3,
        scratch_shapes=[
            vm((chan, rows, LANE), BF),
            vm((rows, LANE), BF),
            vm((27, channels, channels), BF),
            vm((deep, (height + 2) * LANE), BF),
            vm((9 * pad, height * LANE), BF),
            vm((3, 9 * pad, channels), BF),
            vm((9 * pad, deep), BF),
            vm((3 * channels, 9 * pad), BF),
            vm((3, pad * height, LANE), F32),
            vm((3, pad * height, LANE), F32),
            vm((max(9 * pad, 3 * channels), height * LANE), F32),
            vm((channels * height, LANE), F32),
            vm((2, rows, LANE), BF),
            vm((2, rows, LANE), BF),
            vm((2, rows, LANE), BF),
            tuple(vm((tall, 2 * half), F32) for half in halves),
            tuple(vm((tall, half), BF) for half in halves),
            tuple(vm((tall, half), BF) for half in halves),
            tuple(vm((space, tall, half), BF) for half in halves),
            tuple(vm((2, tall, half), BF) for half in halves),
            tuple(vm((3 * tall, flat), BF) for flat in flats),
            vm((3 * tall, 3 * wide), F32),
            tuple(vm((flat, 3 * wide), BF) for flat in flats),
            vm((chan // 2 + 1, rows, LANE), BF),
            vm((chan // 2 + 1, rows, LANE), BF),
            vm((chan // 2, rows, LANE), BF),
            vm((chan // 2, rows, LANE), BF),
            dma((3,)), dma((chan,)), dma((chan,)), dma((2,)), dma((2,)), dma((2,)), dma((2,)),
            dma((groups,)), dma((groups,)), dma((groups, space)), dma((groups, space)),
            dma((groups,)), dma((groups,)),
            dma((chan // 2 + 1,)), dma((chan // 2 + 1,)), dma((chan // 2,)), dma((chan // 2,)),
        ],
        compiler_params=pltpu.CompilerParams(
            collective_id=0, has_side_effects=True, vmem_limit_bytes=40 * 2**20),
    )(*[pltpu.with_memory_space_constraint(x, pltpu.HBM) for x in (
        activation.reshape(rows, width), cotangent.reshape(rows, width),
        weights.reshape(27, channels, channels))])
    out, back, grads = pl.pallas_call(
        write,
        out_shape=shapes,
        in_specs=[pl.BlockSpec(memory_space=vm)] * 3,
        out_specs=[pl.BlockSpec(memory_space=pltpu.HBM)] * 3,
        scratch_shapes=[dma((3,))],
        compiler_params=pltpu.CompilerParams(vmem_limit_bytes=2**20),
    )(*outs)
    field = (1, blk, height, width)
    grads = jnp.swapaxes(grads.reshape(3, 3, 3, blk, channels), 3, 4)
    return out.reshape(field), back.reshape(field), grads


def solution(mesh):
    field = P("space", "chan", None, None)
    return jax.shard_map(
        functools.partial(body, mesh.shape["space"], mesh.shape["chan"]),
        mesh=mesh,
        in_specs=(field, P(), field),
        out_specs=(field, field, P(None, None, None, None, "chan")),
        check_vma=False,
    )
```
